32 devices in a mesh: tx: 16 (over z, y, x), rx: 2 (over core).
Axes of the slice: x: 2, y: 2, z: 4, core: 2. Of those that a mesh axis runs over, the one named last changes fastest.
Arguments:
- captures: bfloat16 [128, 128, 256], P('tx', 'rx'), may hold values from -6 to 6
- elem_grid: int32 [2, 128], replicated, may hold values from 0 to 31, as said below
- excitation: int32 [64], replicated, may hold values from -1 to 1, as said below
- voxels: int32 [3, 512], replicated, may hold values from 0 to 63
Outputs:
- focused_image: float32 [2, 512], P(None, ('tx', 'rx'))
The draws below stay inside these ranges and needn't reach their ends.
Inputs may be any that keep to these rules, and one draw needn't show every extreme that they name: `elem_grid`: every position of the probe's grid of 4 rows and 32 columns holds exactly one element. `excitation`: each tap is -1 or +1.
All inputs are finite; a program needn't handle non-finite values.
Results may differ from the reference program's by a relative error of at most 0.008.
Values may be sent and summed in bfloat16 or wider, within the bound.
A program may use at most 64 MiB of HBM per device.

```python
import math
import jax
import jax.numpy as jnp
from jax import lax

SUBRUN = 4
GATE = 256
TAPS = 64
BINS = 8
ELEM = 128
VOX = 512
N_TX = 16
N_RX = 2


def draw_elem_grid(key, part):
    key = jax.random.fold_in(key, 11)
    shuffled = jax.random.permutation(key, ELEM)
    return jnp.stack([shuffled // 32, shuffled % 32], axis=0).astype(jnp.int32)


def draw_excitation(key, part):
    key = jax.random.fold_in(key, 23)
    coin_flips = jax.random.randint(key, (TAPS,), 0, 2)
    return (2 * coin_flips - 1).astype(jnp.int32)


def plant(entries, own_key, smallest, high):
    longest = entries.shape.index(max(entries.shape))
    spots = []
    for shift in (0, 1):
        where = [jax.random.randint(jax.random.fold_in(own_key, axis), (), 0, length) for axis, length in enumerate(entries.shape)]
        where[longest] = (where[longest] + shift) % entries.shape[longest]
        spots.append(tuple(where))
    return entries.at[spots[0]].set(smallest).at[spots[1]].set(high)


def with_spikes(values, own_key, source, target, blocks, factor):
    def block_of(axis_at):
        return (jnp.arange(values.shape[axis_at]) // (values.shape[axis_at] // blocks)).reshape((-1,) + (1,) * (values.ndim - 1 - axis_at))

    near = jax.random.permutation(own_key, blocks)[block_of(target)]
    other_side = (block_of(target) + blocks // 2) % blocks
    return jnp.where((block_of(source) == near) | (block_of(source) == other_side), factor * values, values)


def levels(key, shape, cuts, least, high):
    def one(axis_at, parts):
        heights = jax.random.uniform(jax.random.fold_in(jax.random.fold_in(key, 6), axis_at), (parts,), jnp.float32, least / len(cuts), high / len(cuts))
        return jnp.repeat(jnp.exp(heights), shape[axis_at] // parts).reshape((-1,) + (1,) * (len(shape) - axis_at - 1))

    gain = one(*cuts[0])
    for cut in cuts[1:]:
        gain = gain * one(*cut)
    return gain


def bell_draw_with(key, shape, width, bound, cuts, heavy, kind=jnp.bfloat16):
    values = width * jax.random.normal(key, shape, jnp.float32)
    if cuts:
        values = values * levels(key, shape, cuts, -0.22, 0.18)
    return jnp.clip(with_spikes(values, jax.random.fold_in(key, 3), *heavy), -bound, bound).astype(kind)


def setup_inputs(seed: int = 0) -> dict:
    seeds = jax.random.split(jax.random.key(seed), 5)
    return {
        "captures": bell_draw_with(seeds[0], (ELEM, ELEM, GATE), 1.0, 6.0, ((0, 16), (1, 2)), (0, 1, 16, 2.0)),
        "elem_grid": draw_elem_grid(jax.random.fold_in(seeds[4], 71), 0),
        "excitation": draw_excitation(jax.random.fold_in(seeds[4], 71), 0),
        "voxels": plant(jax.random.randint(seeds[3], (3, VOX), 0, 64), jax.random.fold_in(seeds[3], 1), 0, 63).astype(jnp.int32),
    }


samples_per_mm = 8.4746
pitch_mm = 0.5
power_floor = 0.1

def filter_table(excitation, gate_len, bin_count):
    tap_count = excitation.shape[0]
    first_bin = gate_len // 12
    lag_index = jnp.arange(gate_len, dtype=jnp.int32)[:, None] - jnp.arange(tap_count, dtype=jnp.int32)[None, :]
    frequency = first_bin + jnp.arange(bin_count, dtype=jnp.int32)
    phase_turns = jnp.mod(lag_index[:, :, None] * frequency[None, None, :], gate_len)
    phases = 2.0 * math.pi / gate_len * phase_turns.astype(jnp.float32)
    weight = jnp.where(lag_index >= 0, excitation[None, :], 0).astype(jnp.float32)[:, :, None]
    norm_scale = 1.0 / math.sqrt(tap_count * gate_len)
    real_part = lax.optimization_barrier(jnp.sum(weight * jnp.cos(phases), axis=1)) * norm_scale
    imag_part = -lax.optimization_barrier(jnp.sum(weight * jnp.sin(phases), axis=1)) * norm_scale
    return jnp.concatenate([real_part, imag_part], axis=1).astype(jnp.bfloat16)

def element_points(grid_cells, grid_rows):
    elem_x = (grid_cells[0].astype(jnp.float32) - 0.5 * (grid_rows - 1)) * pitch_mm
    elem_y = (grid_cells[1].astype(jnp.float32) - 15.5) * pitch_mm
    return (elem_x, elem_y)

def voxel_points(block_cells):
    cells_float = block_cells.astype(jnp.float32)
    return ((cells_float[0] - 31.5) * 0.5, (cells_float[1] - 31.5) * 0.5, 10.0 + cells_float[2] * 0.5)

def steer_angle(elem_x, elem_y, vox_x, vox_y, vox_z, frequency, gate_len):
    distance = jnp.sqrt((elem_x[:, None] - vox_x[None, :]) ** 2 + (elem_y[:, None] - vox_y[None, :]) ** 2 + vox_z[None, :] ** 2)
    delay = distance * (samples_per_mm / gate_len)
    return 2.0 * math.pi * frequency.astype(jnp.float32)[:, None, None] * delay[None]

def bf16_round(values):
    rounded = lax.optimization_barrier(values.astype(jnp.bfloat16))
    return rounded.astype(jnp.float32)

def reference(captures, elem_grid, excitation, voxels):
    matched = filter_table(excitation, GATE, BINS).astype(jnp.float32)
    channels = 2 * BINS
    tx_block = ELEM // N_TX

    def spectra_block(block):
        flattened = block.astype(jnp.float32).reshape(-1, GATE)
        product = jnp.dot(flattened, matched, precision=lax.Precision.HIGHEST)
        return bf16_round(product).reshape(tx_block, ELEM, channels)
    spectra = lax.map(spectra_block, captures.reshape(N_TX, tx_block, ELEM, GATE)).reshape(ELEM, ELEM, channels)
    split_spec = spectra.reshape(N_TX, N_RX, SUBRUN, N_RX, N_TX, SUBRUN, channels)
    mirrored = split_spec.transpose(4, 3, 5, 1, 0, 2, 6).reshape(ELEM, ELEM, channels)
    averaged = (spectra + mirrored) * 0.5
    power = lax.optimization_barrier(jnp.mean(averaged * averaged, axis=2, keepdims=True))
    whitened = bf16_round(averaged / jnp.sqrt(jnp.maximum(power, power_floor)))
    avg_real = jnp.moveaxis(whitened[:, :, :BINS], 2, 0)
    avg_imag = jnp.moveaxis(whitened[:, :, BINS:], 2, 0)
    elem_x, elem_y = element_points(elem_grid, ELEM // 32)
    recv_order = jnp.arange(ELEM, dtype=jnp.int32).reshape(N_TX, N_RX, SUBRUN).transpose(1, 0, 2).reshape(-1)
    recv_x = elem_x[recv_order]
    recv_y = elem_y[recv_order]
    frequency = GATE // 12 + jnp.arange(BINS, dtype=jnp.int32)
    block_width = min(512, VOX)
    voxel_blocks = voxels.reshape(3, VOX // block_width, block_width).transpose(1, 0, 2)
    highest = lax.Precision.HIGHEST

    def image_block(block_cells):
        vox_x, vox_y, vox_z = voxel_points(block_cells)
        recv_phase = steer_angle(recv_x, recv_y, vox_x, vox_y, vox_z, frequency, GATE)
        rx_cosine = bf16_round(jnp.cos(recv_phase))
        rx_sine = bf16_round(jnp.sin(recv_phase))
        prod_real = jnp.einsum('ftj,fjv->ftv', avg_real, rx_cosine, precision=highest) - jnp.einsum('ftj,fjv->ftv', avg_imag, rx_sine, precision=highest)
        prod_imag = jnp.einsum('ftj,fjv->ftv', avg_real, rx_sine, precision=highest) + jnp.einsum('ftj,fjv->ftv', avg_imag, rx_cosine, precision=highest)
        send_phase = steer_angle(elem_x, elem_y, vox_x, vox_y, vox_z, frequency, GATE)
        tx_cosine = jnp.cos(send_phase)
        tx_sine = jnp.sin(send_phase)
        image_real = lax.optimization_barrier(jnp.sum(prod_real * tx_cosine - prod_imag * tx_sine, axis=(0, 1)))
        image_imag = lax.optimization_barrier(jnp.sum(prod_real * tx_sine + prod_imag * tx_cosine, axis=(0, 1)))
        return jnp.stack([image_real, image_imag])
    blocks = lax.map(image_block, voxel_blocks)
    return blocks.transpose(1, 0, 2).reshape(2, VOX) / (ELEM * math.sqrt(BINS))
```

```python
import functools
import math

import jax
import jax.numpy as jnp
import numpy as np
from jax import lax
from jax.experimental import pallas as pl
from jax.experimental.pallas import tpu as pltpu
from jax.sharding import PartitionSpec as P

BINS = 8
LANES = 128


samples_per_mm = 8.4746
pitch_mm = 0.5
power_floor = 0.1


def filter_table(excitation, gate_len, bin_count):
    tap_count = excitation.shape[0]
    first_bin = gate_len // 12
    lag_index = (
        jnp.arange(gate_len, dtype=jnp.int32)[:, None]
        - jnp.arange(tap_count, dtype=jnp.int32)[None, :]
    )
    frequency = first_bin + jnp.arange(bin_count, dtype=jnp.int32)
    phase_turns = jnp.mod(lag_index[:, :, None] * frequency[None, None, :], gate_len)
    phases = 2.0 * math.pi / gate_len * phase_turns.astype(jnp.float32)
    weight = jnp.where(lag_index >= 0, excitation[None, :], 0).astype(jnp.float32)[:, :, None]
    norm_scale = 1.0 / math.sqrt(tap_count * gate_len)
    real_part = jnp.sum(weight * jnp.cos(phases), axis=1) * norm_scale
    imag_part = -jnp.sum(weight * jnp.sin(phases), axis=1) * norm_scale
    return jnp.concatenate([real_part, imag_part], axis=1).astype(jnp.bfloat16)


def element_points(grid_cells, grid_rows):
    elem_x = (grid_cells[0].astype(jnp.float32) - 0.5 * (grid_rows - 1)) * pitch_mm
    elem_y = (grid_cells[1].astype(jnp.float32) - 15.5) * pitch_mm
    return (elem_x, elem_y)


def voxel_points(block_cells):
    cells_float = block_cells.astype(jnp.float32)
    return (
        (cells_float[0] - 31.5) * 0.5,
        (cells_float[1] - 31.5) * 0.5,
        10.0 + cells_float[2] * 0.5,
    )


def steer_angle(elem_x, elem_y, vox_x, vox_y, vox_z, frequency, gate_len):
    distance = jnp.sqrt(
        (elem_x[:, None] - vox_x[None, :]) ** 2
        + (elem_y[:, None] - vox_y[None, :]) ** 2
        + vox_z[None, :] ** 2
    )
    delay = distance * (samples_per_mm / gate_len)
    return 2.0 * math.pi * frequency.astype(jnp.float32)[:, None, None] * delay[None]


def general(captures, elem_grid, excitation, voxels):
    tx_count = lax.axis_size("tx")
    rx_count = lax.axis_size("rx")
    tx_rows, rx_cols, gate_len = captures.shape
    subrun = rx_cols // tx_count
    channels = 2 * BINS
    elements = tx_rows * tx_count
    matched = filter_table(excitation, gate_len, BINS)
    pieces = captures.reshape(rx_count, subrun, tx_count, subrun, gate_len)
    local_spec = jnp.einsum(
        "bhaxs,sc->cbhax", pieces, matched, preferred_element_type=jnp.float32
    ).astype(jnp.bfloat16)
    arrived = lax.all_to_all(
        lax.all_to_all(pieces, "tx", split_axis=2, concat_axis=2, tiled=True),
        "rx",
        split_axis=0,
        concat_axis=0,
        tiled=True,
    )
    mirror = jnp.einsum(
        "bhgxs,sc->cbxgh", arrived, matched, preferred_element_type=jnp.float32
    ).astype(jnp.bfloat16)
    averaged = ((local_spec.astype(jnp.float32) + mirror.astype(jnp.float32)) * 0.5).reshape(
        channels, tx_rows, rx_cols
    )
    power = jnp.mean(averaged * averaged, axis=0, keepdims=True)
    whitened = (
        (averaged / jnp.sqrt(jnp.maximum(power, power_floor)))
        .astype(jnp.bfloat16)
        .reshape(2, BINS, tx_rows, rx_cols)
    )
    left_side = jnp.concatenate([whitened[0], whitened[1]], axis=2)
    tx_cells = lax.dynamic_slice_in_dim(elem_grid, lax.axis_index("tx") * tx_rows, tx_rows, axis=1)
    rx_cells = lax.dynamic_index_in_dim(
        elem_grid.reshape(2, tx_count, rx_count, subrun),
        lax.axis_index("rx"),
        axis=2,
        keepdims=False,
    ).reshape(2, rx_cols)
    send_x, send_y = element_points(tx_cells, elements // 32)
    recv_x, recv_y = element_points(rx_cells, elements // 32)
    frequency = gate_len // 12 + jnp.arange(BINS, dtype=jnp.int32)
    voxel_count = voxels.shape[1]
    block_width = min(512, voxel_count)
    voxel_blocks = voxels.reshape(3, voxel_count // block_width, block_width).transpose(1, 0, 2)

    def image_block(block_cells):
        vox_x, vox_y, vox_z = voxel_points(block_cells)
        recv_phase = steer_angle(recv_x, recv_y, vox_x, vox_y, vox_z, frequency, gate_len)
        rx_cosine = jnp.cos(recv_phase).astype(jnp.bfloat16)
        rx_sine = jnp.sin(recv_phase).astype(jnp.bfloat16)
        steer_rx = jnp.concatenate(
            [
                jnp.concatenate([rx_cosine, rx_sine], axis=2),
                jnp.concatenate([-rx_sine, rx_cosine], axis=2),
            ],
            axis=1,
        )
        products = jnp.einsum(
            "ftl,flv->ftv", left_side, steer_rx, preferred_element_type=jnp.float32
        )
        prod_real = products[:, :, :block_width]
        prod_imag = products[:, :, block_width:]
        send_phase = steer_angle(send_x, send_y, vox_x, vox_y, vox_z, frequency, gate_len)
        tx_cosine = jnp.cos(send_phase)
        tx_sine = jnp.sin(send_phase)
        image_real = jnp.sum(prod_real * tx_cosine - prod_imag * tx_sine, axis=(0, 1))
        image_imag = jnp.sum(prod_real * tx_sine + prod_imag * tx_cosine, axis=(0, 1))
        return jnp.stack([image_real, image_imag])

    blocks = lax.map(image_block, voxel_blocks)
    partial_value = blocks.transpose(1, 0, 2).reshape(2, voxel_count) * (
        1.0 / (elements * math.sqrt(BINS))
    )
    image_part = lax.psum_scatter(partial_value, ("tx", "rx"), scatter_dimension=1, tiled=True)
    return image_part


def cosine_fit():
    grid = np.cos(np.pi * (np.arange(400) + 0.5) / 400) * 0.125 + 0.125
    fit = np.polynomial.chebyshev.Chebyshev.fit(
        grid, np.cos(2.0 * np.pi * np.sqrt(grid)), 8, domain=[0.0, 0.25]
    )
    return [float(c) for c in fit.convert(kind=np.polynomial.Polynomial).coef]


COSINE = cosine_fit()


def cos_turns(turns):
    rest = turns - jnp.floor(turns + 0.5)
    square = rest * rest
    total = jnp.full_like(square, COSINE[-1])
    for factor in COSINE[-2::-1]:
        total = total * square + factor
    return total


def iota(shape, axis):
    return lax.broadcasted_iota(jnp.int32, shape, axis)


def one_hot(mask):
    return jnp.where(mask, 1.0, 0.0).astype(jnp.bfloat16)


def matmul(left, right):
    return jnp.dot(left, right, preferred_element_type=jnp.float32)


def filter_lanes(excitation, gate_len):
    taps = excitation.shape[1]
    first_bin = gate_len // 12

    def turns(rows):
        lane = iota((rows, LANES), 1)
        step = iota((rows, LANES), 0) * (first_bin + (lane & (BINS - 1)))
        return (step & (gate_len - 1)).astype(jnp.float32) * (1.0 / gate_len), lane

    tap_turns, _ = turns(taps)
    tables = jnp.concatenate([cos_turns(tap_turns), cos_turns(tap_turns - 0.25)], axis=1)
    high = tables.astype(jnp.bfloat16)
    rest = tables - high.astype(jnp.float32)
    middle = rest.astype(jnp.bfloat16)
    low = (rest - middle.astype(jnp.float32)).astype(jnp.bfloat16)
    reached = iota((gate_len, taps), 1) <= iota((gate_len, taps), 0)
    weight = jnp.where(reached, excitation.astype(jnp.float32), 0.0).astype(jnp.bfloat16)
    sums = matmul(weight, high) + (matmul(weight, middle) + matmul(weight, low))
    gate_turns, lane = turns(gate_len)
    gate_turns = gate_turns + jnp.where((lane & BINS) != 0, 0.25, 0.0)
    table = cos_turns(gate_turns) * sums[:, :LANES] + cos_turns(gate_turns - 0.25) * sums[:, LANES:]
    return (table * (1.0 / math.sqrt(taps * gate_len))).astype(jnp.bfloat16)


def steer_rows(elem_x, elem_y, points, gate_len, quarter, store):
    middle = gate_len // 12 + BINS // 2
    distance = jnp.sqrt(
        (elem_x - points[0]) ** 2 + (elem_y - points[1]) ** 2 + points[2] ** 2
    )
    turns = distance * (samples_per_mm / gate_len)
    twice = 2.0 * cos_turns(turns)
    for kind in range(2):
        back = 0.25 * kind
        now = cos_turns(turns * middle - back)
        before = cos_turns(turns * (middle - 1) - back)
        store(kind, BINS // 2, now)
        store(kind, BINS // 2 - 1, before)
        low, high = before, now
        for f in range(BINS // 2 - 2, -1, -1):
            low, high = twice * low - high, low
            store(kind, f, low)
        low, high = before, now
        for f in range(BINS // 2 + 1, BINS):
            low, high = high, twice * high - low
            store(kind, f, high)


def kernel(
    tx_count,
    rx_count,
    cap_any,
    grid_any,
    exc_any,
    vox_any,
    out_ref,
    cap,
    grid,
    exc,
    vox,
    steer_rx,
    steer_tx,
    send_spec,
    recv_spec,
    send_part,
    recv_part,
    load_sems,
    spec_sems,
    part_sems,
):
    devices = tx_count * rx_count
    tx_rows, rx_cols, gate_len = cap.shape
    subrun = rx_cols // tx_count
    channels = 2 * BINS
    width = subrun * subrun * channels
    voxel_count = vox.shape[1]
    owned = voxel_count // devices
    me_tx, me_rx = lax.axis_index("tx"), lax.axis_index("rx")
    me = me_tx * rx_count + me_rx
    slot = me_rx * tx_count + me_tx

    loads = [
        pltpu.make_async_copy(source, target, load_sems.at[i])
        for i, (source, target) in enumerate(
            ((exc_any, exc), (cap_any, cap), (grid_any, grid), (vox_any, vox))
        )
    ]
    for load in loads:
        load.start()

    def partner(i):
        other = lax.rem(me + i, devices)
        return other, lax.div(other, rx_count), lax.rem(other, rx_count)

    barrier = pltpu.get_barrier_semaphore()

    @pl.loop(1, devices)
    def _(i):
        _, tx, rx = partner(i)
        pl.semaphore_signal(
            barrier, inc=1, device_id=(tx, rx), device_id_type=pl.DeviceIdType.MESH
        )

    loads[0].wait()
    table = filter_lanes(exc[...], gate_len)
    table = jnp.concatenate([table] * (width // LANES), axis=1)
    loads[1].wait()
    group = iota((rx_cols, width), 1) // channels
    inner = iota((rx_cols, width), 0) & (subrun - 1)
    own_key = group - inner
    sent_key = group - subrun * inner
    rows = []
    for t in range(tx_rows):
        spec = matmul(cap[t], table)
        own = jnp.where(own_key == subrun * (t % subrun), spec, 0.0)
        sent = jnp.where(sent_key == t % subrun, spec, 0.0)
        rows.append(jnp.concatenate([own, sent], axis=1).astype(jnp.bfloat16))
    rows = jnp.concatenate(rows, axis=0)
    pairs = tx_rows * rx_cols
    pair = iota((devices, pairs), 1)
    partner_row = (pair // (rx_cols * subrun)) * tx_count + (pair & (rx_cols - 1)) // subrun
    both = matmul(one_hot(partner_row == iota((devices, pairs), 0)), rows)
    own_spec = both[:, :width]
    send_spec[...] = both[:, width:].reshape(devices, 1, width)
    recv_spec[pl.ds(slot, 1)] = send_spec[pl.ds(slot, 1)]

    pl.semaphore_wait(barrier, devices - 1)

    @pl.loop(1, devices)
    def _(i):
        _, tx, rx = partner(i)
        pltpu.make_async_remote_copy(
            src_ref=send_spec.at[rx * tx_count + tx],
            dst_ref=recv_spec.at[slot],
            send_sem=spec_sems.at[0],
            recv_sem=spec_sems.at[1],
            device_id=(tx, rx),
            device_id_type=pl.DeviceIdType.MESH,
        ).start()

    loads[2].wait()
    loads[3].wait()
    elements = grid.shape[1]
    cells = grid[...].astype(jnp.float32)
    x_line = (cells[0:1] - 0.5 * (elements // 32 - 1)) * pitch_mm
    y_line = (cells[1:2] - 15.5) * pitch_mm
    points = voxel_points(vox[...])
    points = tuple(p.reshape(1, voxel_count) for p in points)

    def columns(chosen):
        return (
            jnp.sum(jnp.where(chosen, x_line, 0.0), axis=1, keepdims=True),
            jnp.sum(jnp.where(chosen, y_line, 0.0), axis=1, keepdims=True),
        )

    chunk = 16
    for first in range(0, rx_cols, chunk):
        j = iota((chunk, elements), 0) + first
        element = (j // subrun) * tx_rows + me_rx * subrun + (j & (subrun - 1))
        elem_x, elem_y = columns(iota((chunk, elements), 1) == element)

        def store(kind, f, values, first=first):
            steer_rx[f, pl.ds(kind * rx_cols + first, chunk), :] = values.astype(jnp.bfloat16)

        steer_rows(elem_x, elem_y, points, gate_len, 0, store)
    element = iota((tx_rows, elements), 0) + me_tx * tx_rows
    elem_x, elem_y = columns(iota((tx_rows, elements), 1) == element)

    def store_tx(kind, f, values):
        steer_tx[f, pl.ds(kind * tx_rows, tx_rows), :] = values

    steer_rows(elem_x, elem_y, points, gate_len, 0, store_tx)

    same = one_hot(iota((width, width), 0) // channels == iota((width, width), 1) // channels)
    spread_rows = 2 * rx_cols
    spread = one_hot(
        iota((spread_rows, 2 * tx_count), 0) // subrun == iota((spread_rows, 2 * tx_count), 1)
    )
    long = rx_count * width
    kept = (iota((spread_rows, long), 1) // channels) % subrun == (
        iota((spread_rows, long), 0) & (subrun - 1)
    )
    fold_row = iota((channels * tx_rows, long), 0)
    fold_lane = iota((channels * tx_rows, long), 1)
    fold = one_hot(
        ((fold_row & (tx_rows - 1)) == fold_lane // (subrun * channels))
        & (fold_row // tx_rows == (fold_lane & (BINS - 1)) * 2 + ((fold_lane // BINS) & 1))
    )

    pltpu.make_async_copy(
        recv_spec.at[pl.ds(0, devices - 1)], recv_spec.at[pl.ds(0, devices - 1)], spec_sems.at[1]
    ).wait()
    averaged = (own_spec + recv_spec[...].reshape(devices, width)) * 0.5
    square = averaged * averaged
    high = square.astype(jnp.bfloat16)
    low = (square - high.astype(jnp.float32)).astype(jnp.bfloat16)
    power = (matmul(high, same) + matmul(low, same)) * (1.0 / channels)
    whitened = averaged * lax.rsqrt(jnp.maximum(power, power_floor))
    imag_lane = (iota((devices, width), 1) & BINS) != 0
    turned = jnp.where(
        imag_lane, pltpu.roll(whitened, BINS, 1), -pltpu.roll(whitened, width - BINS, 1)
    )

    def side(values):
        return jnp.concatenate(
            [values[b * tx_count : (b + 1) * tx_count] for b in range(rx_count)], axis=1
        )

    both = jnp.concatenate([side(whitened), side(turned)], axis=0).astype(jnp.bfloat16)
    wide = jnp.where(kept, matmul(spread, both), 0.0).astype(jnp.bfloat16)
    left = lax.dot_general(
        fold, wide, (((1,), (1,)), ((), ())), preferred_element_type=jnp.float32
    ).astype(jnp.bfloat16)
    real = jnp.zeros((tx_rows, voxel_count), jnp.float32)
    imag = jnp.zeros((tx_rows, voxel_count), jnp.float32)
    for f in range(BINS):
        products = matmul(left[2 * tx_rows * f : 2 * tx_rows * (f + 1)], steer_rx[f])
        prod_real, prod_imag = products[:tx_rows], products[tx_rows:]
        tx_cosine, tx_sine = steer_tx[f, :tx_rows, :], steer_tx[f, tx_rows:, :]
        real += prod_real * tx_cosine - prod_imag * tx_sine
        imag += prod_real * tx_sine + prod_imag * tx_cosine
    image = jnp.concatenate(
        [jnp.sum(real, axis=0, keepdims=True), jnp.sum(imag, axis=0, keepdims=True)], axis=0
    ) * (1.0 / (elements * math.sqrt(BINS)))
    for tile in range(voxel_count // LANES):
        send_part[tile] = image[:, tile * LANES : (tile + 1) * LANES]
    per_tile = LANES // owned

    @pl.loop(1, devices)
    def _(i):
        other, tx, rx = partner(i)
        pltpu.make_async_remote_copy(
            src_ref=send_part.at[lax.div(other, per_tile)],
            dst_ref=recv_part.at[me],
            send_sem=part_sems.at[0],
            recv_sem=part_sems.at[1],
            device_id=(tx, rx),
            device_id_type=pl.DeviceIdType.MESH,
        ).start()

    recv_part[pl.ds(me, 1)] = send_part[pl.ds(lax.div(me, per_tile), 1)]
    all_but_one = recv_part.at[pl.ds(0, devices - 1)]
    pltpu.make_async_copy(all_but_one, all_but_one, part_sems.at[1]).wait()
    total = jnp.sum(recv_part[...], axis=0)
    shift = lax.rem(LANES - owned * lax.rem(me, per_tile), LANES)
    out_ref[...] = pltpu.roll(total, shift, 1)[:, :owned]
    sent_spec = send_spec.at[pl.ds(0, devices - 1)]
    pltpu.make_async_copy(sent_spec, sent_spec, spec_sems.at[0]).wait()
    pltpu.make_async_copy(all_but_one, all_but_one, part_sems.at[0]).wait()


def small(captures, elem_grid, excitation, voxels):
    tx_count = lax.axis_size("tx")
    rx_count = lax.axis_size("rx")
    devices = tx_count * rx_count
    tx_rows, rx_cols, gate_len = captures.shape
    voxel_count = voxels.shape[1]
    width = (rx_cols // tx_count) ** 2 * 2 * BINS
    excitation = excitation.reshape(1, -1)
    return pl.pallas_call(
        functools.partial(kernel, tx_count, rx_count),
        out_shape=jax.ShapeDtypeStruct((2, voxel_count // devices), jnp.float32),
        in_specs=[pl.BlockSpec(memory_space=pl.ANY)] * 4,
        out_specs=pl.BlockSpec(memory_space=pltpu.VMEM),
        scratch_shapes=[
            pltpu.VMEM(captures.shape, captures.dtype),
            pltpu.VMEM(elem_grid.shape, jnp.int32),
            pltpu.VMEM(excitation.shape, jnp.int32),
            pltpu.VMEM(voxels.shape, jnp.int32),
            pltpu.VMEM((BINS, 2 * rx_cols, voxel_count), jnp.bfloat16),
            pltpu.VMEM((BINS, 2 * tx_rows, voxel_count), jnp.float32),
            pltpu.VMEM((devices, 1, width), jnp.float32),
            pltpu.VMEM((devices, 1, width), jnp.float32),
            pltpu.VMEM((voxel_count // LANES, 2, LANES), jnp.float32),
            pltpu.VMEM((devices, 2, LANES), jnp.float32),
            pltpu.SemaphoreType.DMA((4,)),
            pltpu.SemaphoreType.DMA((2,)),
            pltpu.SemaphoreType.DMA((2,)),
        ],
        compiler_params=pltpu.CompilerParams(
            collective_id=0, has_side_effects=True, vmem_limit_bytes=32 * 1024 * 1024
        ),
    )(captures, elem_grid, excitation, voxels)


def local(captures, elem_grid, excitation, voxels):
    tx_count = lax.axis_size("tx")
    devices = tx_count * lax.axis_size("rx")
    tx_rows, rx_cols, _ = captures.shape
    fits = (
        tx_rows == 8
        and rx_cols == 64
        and rx_cols // tx_count == 4
        and voxels.shape[1] <= 1024
        and LANES % (voxels.shape[1] // devices) == 0
    )
    return (small if fits else general)(captures, elem_grid, excitation, voxels)


def solution(mesh):
    placed = (P("tx", "rx", None), P(), P(), P())
    return jax.shard_map(
        local, mesh=mesh, in_specs=placed, out_specs=P(None, ("tx", "rx")), check_vma=False
    )
```

```python
import functools
import math

import jax
import jax.numpy as jnp
import numpy as np
from jax import lax
from jax.experimental import pallas as pl
from jax.experimental.pallas import tpu as pltpu
from jax.sharding import PartitionSpec as P

BINS = 8
LANES = 128


samples_per_mm = 8.4746
pitch_mm = 0.5
power_floor = 0.1


def filter_table(excitation, gate_len, bin_count):
    tap_count = excitation.shape[0]
    first_bin = gate_len // 12
    lag_index = (
        jnp.arange(gate_len, dtype=jnp.int32)[:, None]
        - jnp.arange(tap_count, dtype=jnp.int32)[None, :]
    )
    frequency = first_bin + jnp.arange(bin_count, dtype=jnp.int32)
    phase_turns = jnp.mod(lag_index[:, :, None] * frequency[None, None, :], gate_len)
    phases = 2.0 * math.pi / gate_len * phase_turns.astype(jnp.float32)
    weight = jnp.where(lag_index >= 0, excitation[None, :], 0).astype(jnp.float32)[:, :, None]
    norm_scale = 1.0 / math.sqrt(tap_count * gate_len)
    real_part = jnp.sum(weight * jnp.cos(phases), axis=1) * norm_scale
    imag_part = -jnp.sum(weight * jnp.sin(phases), axis=1) * norm_scale
    return jnp.concatenate([real_part, imag_part], axis=1).astype(jnp.bfloat16)


def element_points(grid_cells, grid_rows):
    elem_x = (grid_cells[0].astype(jnp.float32) - 0.5 * (grid_rows - 1)) * pitch_mm
    elem_y = (grid_cells[1].astype(jnp.float32) - 15.5) * pitch_mm
    return (elem_x, elem_y)


def voxel_points(block_cells):
    cells_float = block_cells.astype(jnp.float32)
    return (
        (cells_float[0] - 31.5) * 0.5,
        (cells_float[1] - 31.5) * 0.5,
        10.0 + cells_float[2] * 0.5,
    )


def steer_angle(elem_x, elem_y, vox_x, vox_y, vox_z, frequency, gate_len):
    distance = jnp.sqrt(
        (elem_x[:, None] - vox_x[None, :]) ** 2
        + (elem_y[:, None] - vox_y[None, :]) ** 2
        + vox_z[None, :] ** 2
    )
    delay = distance * (samples_per_mm / gate_len)
    return 2.0 * math.pi * frequency.astype(jnp.float32)[:, None, None] * delay[None]


def general(captures, elem_grid, excitation, voxels):
    tx_count = lax.axis_size("tx")
    rx_count = lax.axis_size("rx")
    tx_rows, rx_cols, gate_len = captures.shape
    subrun = rx_cols // tx_count
    channels = 2 * BINS
    elements = tx_rows * tx_count
    matched = filter_table(excitation, gate_len, BINS)
    pieces = captures.reshape(rx_count, subrun, tx_count, subrun, gate_len)
    local_spec = jnp.einsum(
        "bhaxs,sc->cbhax", pieces, matched, preferred_element_type=jnp.float32
    ).astype(jnp.bfloat16)
    arrived = lax.all_to_all(
        lax.all_to_all(pieces, "tx", split_axis=2, concat_axis=2, tiled=True),
        "rx",
        split_axis=0,
        concat_axis=0,
        tiled=True,
    )
    mirror = jnp.einsum(
        "bhgxs,sc->cbxgh", arrived, matched, preferred_element_type=jnp.float32
    ).astype(jnp.bfloat16)
    averaged = ((local_spec.astype(jnp.float32) + mirror.astype(jnp.float32)) * 0.5).reshape(
        channels, tx_rows, rx_cols
    )
    power = jnp.mean(averaged * averaged, axis=0, keepdims=True)
    whitened = (
        (averaged / jnp.sqrt(jnp.maximum(power, power_floor)))
        .astype(jnp.bfloat16)
        .reshape(2, BINS, tx_rows, rx_cols)
    )
    left_side = jnp.concatenate([whitened[0], whitened[1]], axis=2)
    tx_cells = lax.dynamic_slice_in_dim(elem_grid, lax.axis_index("tx") * tx_rows, tx_rows, axis=1)
    rx_cells = lax.dynamic_index_in_dim(
        elem_grid.reshape(2, tx_count, rx_count, subrun),
        lax.axis_index("rx"),
        axis=2,
        keepdims=False,
    ).reshape(2, rx_cols)
    send_x, send_y = element_points(tx_cells, elements // 32)
    recv_x, recv_y = element_points(rx_cells, elements // 32)
    frequency = gate_len // 12 + jnp.arange(BINS, dtype=jnp.int32)
    voxel_count = voxels.shape[1]
    block_width = min(512, voxel_count)
    voxel_blocks = voxels.reshape(3, voxel_count // block_width, block_width).transpose(1, 0, 2)

    def image_block(block_cells):
        vox_x, vox_y, vox_z = voxel_points(block_cells)
        recv_phase = steer_angle(recv_x, recv_y, vox_x, vox_y, vox_z, frequency, gate_len)
        rx_cosine = jnp.cos(recv_phase).astype(jnp.bfloat16)
        rx_sine = jnp.sin(recv_phase).astype(jnp.bfloat16)
        steer_rx = jnp.concatenate(
            [
                jnp.concatenate([rx_cosine, rx_sine], axis=2),
                jnp.concatenate([-rx_sine, rx_cosine], axis=2),
            ],
            axis=1,
        )
        products = jnp.einsum(
            "ftl,flv->ftv", left_side, steer_rx, preferred_element_type=jnp.float32
        )
        prod_real = products[:, :, :block_width]
        prod_imag = products[:, :, block_width:]
        send_phase = steer_angle(send_x, send_y, vox_x, vox_y, vox_z, frequency, gate_len)
        tx_cosine = jnp.cos(send_phase)
        tx_sine = jnp.sin(send_phase)
        image_real = jnp.sum(prod_real * tx_cosine - prod_imag * tx_sine, axis=(0, 1))
        image_imag = jnp.sum(prod_real * tx_sine + prod_imag * tx_cosine, axis=(0, 1))
        return jnp.stack([image_real, image_imag])

    blocks = lax.map(image_block, voxel_blocks)
    partial_value = blocks.transpose(1, 0, 2).reshape(2, voxel_count) * (
        1.0 / (elements * math.sqrt(BINS))
    )
    image_part = lax.psum_scatter(partial_value, ("tx", "rx"), scatter_dimension=1, tiled=True)
    return image_part


def cosine_fit():
    grid = np.cos(np.pi * (np.arange(400) + 0.5) / 400) * 0.125 + 0.125
    fit = np.polynomial.chebyshev.Chebyshev.fit(
        grid, np.cos(2.0 * np.pi * np.sqrt(grid)), 8, domain=[0.0, 0.25]
    )
    return [float(c) for c in fit.convert(kind=np.polynomial.Polynomial).coef]


COSINE = cosine_fit()


def cos_turns(turns):
    rest = turns - jnp.floor(turns + 0.5)
    square = rest * rest
    total = jnp.full_like(square, COSINE[-1])
    for factor in COSINE[-2::-1]:
        total = total * square + factor
    return total


def iota(shape, axis):
    return lax.broadcasted_iota(jnp.int32, shape, axis)


def one_hot(mask):
    return jnp.where(mask, 1.0, 0.0).astype(jnp.bfloat16)


def matmul(left, right):
    return jnp.dot(left, right, preferred_element_type=jnp.float32)


def filter_lanes(taps, gate_len):
    first_bin = gate_len // 12

    def turns(rows):
        lane = iota((rows, LANES), 1)
        step = iota((rows, LANES), 0) * (first_bin + (lane & (BINS - 1)))
        return (step & (gate_len - 1)).astype(jnp.float32) * (1.0 / gate_len), lane

    tap_turns, _ = turns(taps)
    tables = jnp.concatenate([cos_turns(tap_turns), cos_turns(tap_turns - 0.25)], axis=1)
    high = tables.astype(jnp.bfloat16)
    rest = tables - high.astype(jnp.float32)
    middle = rest.astype(jnp.bfloat16)
    low = (rest - middle.astype(jnp.float32)).astype(jnp.bfloat16)
    reached = iota((gate_len, taps), 1) <= iota((gate_len, taps), 0)
    gate_turns, lane = turns(gate_len)
    gate_turns = gate_turns + jnp.where((lane & BINS) != 0, 0.25, 0.0)
    scale = 1.0 / math.sqrt(taps * gate_len)
    by_cosine = cos_turns(gate_turns) * scale
    by_sine = cos_turns(gate_turns - 0.25) * scale

    def table(excitation):
        weight = jnp.where(reached, excitation.astype(jnp.float32), 0.0).astype(jnp.bfloat16)
        sums = matmul(weight, high) + (matmul(weight, middle) + matmul(weight, low))
        return (by_cosine * sums[:, :LANES] + by_sine * sums[:, LANES:]).astype(jnp.bfloat16)

    return table


def steer_rows(elem_x, elem_y, points, gate_len, quarter, store):
    middle = gate_len // 12 + BINS // 2
    distance = jnp.sqrt(
        (elem_x - points[0]) ** 2 + (elem_y - points[1]) ** 2 + points[2] ** 2
    )
    turns = distance * (samples_per_mm / gate_len)
    twice = 2.0 * cos_turns(turns)
    for kind in range(2):
        back = 0.25 * kind
        now = cos_turns(turns * middle - back)
        before = cos_turns(turns * (middle - 1) - back)
        store(kind, BINS // 2, now)
        store(kind, BINS // 2 - 1, before)
        low, high = before, now
        for f in range(BINS // 2 - 2, -1, -1):
            low, high = twice * low - high, low
            store(kind, f, low)
        low, high = before, now
        for f in range(BINS // 2 + 1, BINS):
            low, high = high, twice * high - low
            store(kind, f, high)


def kernel(
    tx_count,
    rx_count,
    cap_any,
    grid_any,
    exc_any,
    vox_any,
    out_ref,
    cap,
    grid,
    exc,
    vox,
    steer_rx,
    steer_tx,
    send_spec,
    recv_spec,
    send_part,
    recv_part,
    load_sems,
    spec_sems,
    part_sems,
):
    devices = tx_count * rx_count
    tx_rows, rx_cols, gate_len = cap.shape
    subrun = rx_cols // tx_count
    channels = 2 * BINS
    width = subrun * subrun * channels
    voxel_count = vox.shape[1]
    owned = voxel_count // devices
    me_tx, me_rx = lax.axis_index("tx"), lax.axis_index("rx")
    me = me_tx * rx_count + me_rx
    slot = me_rx * tx_count + me_tx

    loads = [
        pltpu.make_async_copy(source, target, load_sems.at[i])
        for i, (source, target) in enumerate(
            ((exc_any, exc), (cap_any, cap), (grid_any, grid), (vox_any, vox))
        )
    ]
    for load in loads:
        load.start()

    def place(other):
        return lax.div(other, rx_count), lax.rem(other, rx_count)

    def wait_rows(ref, semaphore, count):
        for rows in range(1, devices):

            @pl.when(count == rows)
            def _(rows=rows):
                some = ref.at[pl.ds(0, rows)]
                pltpu.make_async_copy(some, some, semaphore).wait()

    barrier = pltpu.get_barrier_semaphore()

    @pl.loop(me + 1, devices)
    def _(other):
        pl.semaphore_signal(
            barrier, inc=1, device_id=place(other), device_id_type=pl.DeviceIdType.MESH
        )

    make_table = filter_lanes(exc.shape[1], gate_len)
    group = iota((rx_cols, width), 1) // channels
    inner = iota((rx_cols, width), 0) & (subrun - 1)
    own_key = group - inner
    sent_key = group - subrun * inner
    pairs = tx_rows * rx_cols
    pair = iota((devices, pairs), 1)
    partner_row = (pair // (rx_cols * subrun)) * tx_count + (pair & (rx_cols - 1)) // subrun
    gather = one_hot(partner_row == iota((devices, pairs), 0))
    loads[0].wait()
    table = make_table(exc[...])
    table = jnp.concatenate([table] * (width // LANES), axis=1)
    loads[1].wait()
    rows = []
    for t in range(tx_rows):
        spec = matmul(cap[t], table)
        own = jnp.where(own_key == subrun * (t % subrun), spec, 0.0)
        sent = jnp.where(sent_key == t % subrun, spec, 0.0)
        rows.append(jnp.concatenate([own, sent], axis=1).astype(jnp.bfloat16))
    rows = jnp.concatenate(rows, axis=0)
    both = matmul(gather, rows)
    own_spec = both[:, :width]
    send_spec[...] = both[:, width:].reshape(devices, 1, width)
    recv_spec[pl.ds(slot, 1)] = send_spec[pl.ds(slot, 1)]

    @pl.when(me > 0)
    def _():
        pl.semaphore_wait(barrier, me)

    @pl.loop(0, me)
    def _(other):
        tx, rx = place(other)
        pltpu.make_async_remote_copy(
            src_ref=send_spec.at[rx * tx_count + tx],
            dst_ref=recv_spec.at[slot],
            send_sem=spec_sems.at[0],
            recv_sem=spec_sems.at[1],
            device_id=(tx, rx),
            device_id_type=pl.DeviceIdType.MESH,
        ).start()

    loads[2].wait()
    loads[3].wait()
    elements = grid.shape[1]
    cells = grid[...].astype(jnp.float32)
    x_line = (cells[0:1] - 0.5 * (elements // 32 - 1)) * pitch_mm
    y_line = (cells[1:2] - 15.5) * pitch_mm
    points = voxel_points(vox[...])
    points = tuple(p.reshape(1, voxel_count) for p in points)

    def columns(chosen):
        return (
            jnp.sum(jnp.where(chosen, x_line, 0.0), axis=1, keepdims=True),
            jnp.sum(jnp.where(chosen, y_line, 0.0), axis=1, keepdims=True),
        )

    chunk = 16
    for first in range(0, rx_cols, chunk):
        j = iota((chunk, elements), 0) + first
        element = (j // subrun) * tx_rows + me_rx * subrun + (j & (subrun - 1))
        elem_x, elem_y = columns(iota((chunk, elements), 1) == element)

        def store(kind, f, values, first=first):
            steer_rx[f, pl.ds(kind * rx_cols + first, chunk), :] = values.astype(jnp.bfloat16)

        steer_rows(elem_x, elem_y, points, gate_len, 0, store)
    element = iota((tx_rows, elements), 0) + me_tx * tx_rows
    elem_x, elem_y = columns(iota((tx_rows, elements), 1) == element)

    def store_tx(kind, f, values):
        steer_tx[f, pl.ds(kind * tx_rows, tx_rows), :] = values

    steer_rows(elem_x, elem_y, points, gate_len, 0, store_tx)

    same = one_hot(iota((width, width), 0) // channels == iota((width, width), 1) // channels)
    spread_rows = 2 * rx_cols
    spread = one_hot(
        iota((spread_rows, 2 * tx_count), 0) // subrun == iota((spread_rows, 2 * tx_count), 1)
    )
    long = rx_count * width
    kept = (iota((spread_rows, long), 1) // channels) % subrun == (
        iota((spread_rows, long), 0) & (subrun - 1)
    )
    fold_row = iota((channels * tx_rows, long), 0)
    fold_lane = iota((channels * tx_rows, long), 1)
    fold = one_hot(
        ((fold_row & (tx_rows - 1)) == fold_lane // (subrun * channels))
        & (fold_row // tx_rows == (fold_lane & (BINS - 1)) * 2 + ((fold_lane // BINS) & 1))
    )

    row = iota((devices, width), 0)
    sender = lax.rem(row, tx_count) * rx_count + lax.div(row, tx_count)
    times = jnp.where(sender > me, 2.0, 1.0)
    used = sender >= me
    imag_lane = (iota((devices, width), 1) & BINS) != 0

    wait_rows(recv_spec, spec_sems.at[1], devices - 1 - me)
    averaged = jnp.where(used, own_spec + recv_spec[...].reshape(devices, width), 0.0) * 0.5
    square = averaged * averaged
    high = square.astype(jnp.bfloat16)
    low = (square - high.astype(jnp.float32)).astype(jnp.bfloat16)
    power = (matmul(high, same) + matmul(low, same)) * (1.0 / channels)
    whitened = averaged * lax.rsqrt(jnp.maximum(power, power_floor)) * times
    turned = jnp.where(
        imag_lane, pltpu.roll(whitened, BINS, 1), -pltpu.roll(whitened, width - BINS, 1)
    )

    def side(values):
        return jnp.concatenate(
            [values[b * tx_count : (b + 1) * tx_count] for b in range(rx_count)], axis=1
        )

    both = jnp.concatenate([side(whitened), side(turned)], axis=0).astype(jnp.bfloat16)
    wide = jnp.where(kept, matmul(spread, both), 0.0).astype(jnp.bfloat16)
    left = lax.dot_general(
        fold, wide, (((1,), (1,)), ((), ())), preferred_element_type=jnp.float32
    ).astype(jnp.bfloat16)
    real = jnp.zeros((tx_rows, voxel_count), jnp.float32)
    imag = jnp.zeros((tx_rows, voxel_count), jnp.float32)
    for f in range(BINS):
        products = matmul(left[2 * tx_rows * f : 2 * tx_rows * (f + 1)], steer_rx[f])
        prod_real, prod_imag = products[:tx_rows], products[tx_rows:]
        tx_cosine, tx_sine = steer_tx[f, :tx_rows, :], steer_tx[f, tx_rows:, :]
        real += prod_real * tx_cosine - prod_imag * tx_sine
        imag += prod_real * tx_sine + prod_imag * tx_cosine
    image = jnp.concatenate(
        [jnp.sum(real, axis=0, keepdims=True), jnp.sum(imag, axis=0, keepdims=True)], axis=0
    ) * (1.0 / (elements * math.sqrt(BINS)))
    for tile in range(voxel_count // LANES):
        send_part[tile] = image[:, tile * LANES : (tile + 1) * LANES]
    per_tile = LANES // owned

    @pl.loop(0, devices - 1)
    def _(i):
        other = i + jnp.where(i >= me, 1, 0)
        tx, rx = place(other)
        pltpu.make_async_remote_copy(
            src_ref=send_part.at[lax.div(other, per_tile)],
            dst_ref=recv_part.at[me],
            send_sem=part_sems.at[0],
            recv_sem=part_sems.at[1],
            device_id=(tx, rx),
            device_id_type=pl.DeviceIdType.MESH,
        ).start()

    recv_part[pl.ds(me, 1)] = send_part[pl.ds(lax.div(me, per_tile), 1)]
    all_but_one = recv_part.at[pl.ds(0, devices - 1)]
    pltpu.make_async_copy(all_but_one, all_but_one, part_sems.at[1]).wait()
    total = jnp.sum(recv_part[...], axis=0)
    shift = lax.rem(LANES - owned * lax.rem(me, per_tile), LANES)
    out_ref[...] = pltpu.roll(total, shift, 1)[:, :owned]
    wait_rows(send_spec, spec_sems.at[0], me)
    pltpu.make_async_copy(all_but_one, all_but_one, part_sems.at[0]).wait()


def small(captures, elem_grid, excitation, voxels):
    tx_count = lax.axis_size("tx")
    rx_count = lax.axis_size("rx")
    devices = tx_count * rx_count
    tx_rows, rx_cols, gate_len = captures.shape
    voxel_count = voxels.shape[1]
    width = (rx_cols // tx_count) ** 2 * 2 * BINS
    excitation = excitation.reshape(1, -1)
    return pl.pallas_call(
        functools.partial(kernel, tx_count, rx_count),
        out_shape=jax.ShapeDtypeStruct((2, voxel_count // devices), jnp.float32),
        in_specs=[pl.BlockSpec(memory_space=pltpu.HBM)] * 4,
        out_specs=pl.BlockSpec(memory_space=pltpu.VMEM),
        scratch_shapes=[
            pltpu.VMEM(captures.shape, captures.dtype),
            pltpu.VMEM(elem_grid.shape, jnp.int32),
            pltpu.VMEM(excitation.shape, jnp.int32),
            pltpu.VMEM(voxels.shape, jnp.int32),
            pltpu.VMEM((BINS, 2 * rx_cols, voxel_count), jnp.bfloat16),
            pltpu.VMEM((BINS, 2 * tx_rows, voxel_count), jnp.float32),
            pltpu.VMEM((devices, 1, width), jnp.float32),
            pltpu.VMEM((devices, 1, width), jnp.float32),
            pltpu.VMEM((voxel_count // LANES, 2, LANES), jnp.float32),
            pltpu.VMEM((devices, 2, LANES), jnp.float32),
            pltpu.SemaphoreType.DMA((4,)),
            pltpu.SemaphoreType.DMA((2,)),
            pltpu.SemaphoreType.DMA((2,)),
        ],
        compiler_params=pltpu.CompilerParams(
            collective_id=0, has_side_effects=True
        ),
    )(captures, elem_grid, excitation, voxels)


def local(captures, elem_grid, excitation, voxels):
    tx_count = lax.axis_size("tx")
    devices = tx_count * lax.axis_size("rx")
    tx_rows, rx_cols, _ = captures.shape
    fits = (
        tx_rows == 8
        and rx_cols == 64
        and rx_cols // tx_count == 4
        and voxels.shape[1] <= 1024
        and LANES % (voxels.shape[1] // devices) == 0
    )
    return (small if fits else general)(captures, elem_grid, excitation, voxels)


def solution(mesh):
    placed = (P("tx", "rx", None), P(), P(), P())
    return jax.shard_map(
        local, mesh=mesh, in_specs=placed, out_specs=P(None, ("tx", "rx")), check_vma=False
    )
```

```python
import functools
import math

import jax
import jax.numpy as jnp
import numpy as np
from jax import lax
from jax.experimental import pallas as pl
from jax.experimental.pallas import tpu as pltpu
from jax.sharding import PartitionSpec as P

BINS = 8
LANES = 128


samples_per_mm = 8.4746
pitch_mm = 0.5
power_floor = 0.1


def filter_table(excitation, gate_len, bin_count):
    tap_count = excitation.shape[0]
    first_bin = gate_len // 12
    lag_index = (
        jnp.arange(gate_len, dtype=jnp.int32)[:, None]
        - jnp.arange(tap_count, dtype=jnp.int32)[None, :]
    )
    frequency = first_bin + jnp.arange(bin_count, dtype=jnp.int32)
    phase_turns = jnp.mod(lag_index[:, :, None] * frequency[None, None, :], gate_len)
    phases = 2.0 * math.pi / gate_len * phase_turns.astype(jnp.float32)
    weight = jnp.where(lag_index >= 0, excitation[None, :], 0).astype(jnp.float32)[:, :, None]
    norm_scale = 1.0 / math.sqrt(tap_count * gate_len)
    real_part = jnp.sum(weight * jnp.cos(phases), axis=1) * norm_scale
    imag_part = -jnp.sum(weight * jnp.sin(phases), axis=1) * norm_scale
    return jnp.concatenate([real_part, imag_part], axis=1).astype(jnp.bfloat16)


def element_points(grid_cells, grid_rows):
    elem_x = (grid_cells[0].astype(jnp.float32) - 0.5 * (grid_rows - 1)) * pitch_mm
    elem_y = (grid_cells[1].astype(jnp.float32) - 15.5) * pitch_mm
    return (elem_x, elem_y)


def voxel_points(block_cells):
    cells_float = block_cells.astype(jnp.float32)
    return (
        (cells_float[0] - 31.5) * 0.5,
        (cells_float[1] - 31.5) * 0.5,
        10.0 + cells_float[2] * 0.5,
    )


def steer_angle(elem_x, elem_y, vox_x, vox_y, vox_z, frequency, gate_len):
    distance = jnp.sqrt(
        (elem_x[:, None] - vox_x[None, :]) ** 2
        + (elem_y[:, None] - vox_y[None, :]) ** 2
        + vox_z[None, :] ** 2
    )
    delay = distance * (samples_per_mm / gate_len)
    return 2.0 * math.pi * frequency.astype(jnp.float32)[:, None, None] * delay[None]


def general(captures, elem_grid, excitation, voxels):
    tx_count = lax.axis_size("tx")
    rx_count = lax.axis_size("rx")
    tx_rows, rx_cols, gate_len = captures.shape
    subrun = rx_cols // tx_count
    channels = 2 * BINS
    elements = tx_rows * tx_count
    matched = filter_table(excitation, gate_len, BINS)
    pieces = captures.reshape(rx_count, subrun, tx_count, subrun, gate_len)
    local_spec = jnp.einsum(
        "bhaxs,sc->cbhax", pieces, matched, preferred_element_type=jnp.float32
    ).astype(jnp.bfloat16)
    arrived = lax.all_to_all(
        lax.all_to_all(pieces, "tx", split_axis=2, concat_axis=2, tiled=True),
        "rx",
        split_axis=0,
        concat_axis=0,
        tiled=True,
    )
    mirror = jnp.einsum(
        "bhgxs,sc->cbxgh", arrived, matched, preferred_element_type=jnp.float32
    ).astype(jnp.bfloat16)
    averaged = ((local_spec.astype(jnp.float32) + mirror.astype(jnp.float32)) * 0.5).reshape(
        channels, tx_rows, rx_cols
    )
    power = jnp.mean(averaged * averaged, axis=0, keepdims=True)
    whitened = (
        (averaged / jnp.sqrt(jnp.maximum(power, power_floor)))
        .astype(jnp.bfloat16)
        .reshape(2, BINS, tx_rows, rx_cols)
    )
    left_side = jnp.concatenate([whitened[0], whitened[1]], axis=2)
    tx_cells = lax.dynamic_slice_in_dim(elem_grid, lax.axis_index("tx") * tx_rows, tx_rows, axis=1)
    rx_cells = lax.dynamic_index_in_dim(
        elem_grid.reshape(2, tx_count, rx_count, subrun),
        lax.axis_index("rx"),
        axis=2,
        keepdims=False,
    ).reshape(2, rx_cols)
    send_x, send_y = element_points(tx_cells, elements // 32)
    recv_x, recv_y = element_points(rx_cells, elements // 32)
    frequency = gate_len // 12 + jnp.arange(BINS, dtype=jnp.int32)
    voxel_count = voxels.shape[1]
    block_width = min(512, voxel_count)
    voxel_blocks = voxels.reshape(3, voxel_count // block_width, block_width).transpose(1, 0, 2)

    def image_block(block_cells):
        vox_x, vox_y, vox_z = voxel_points(block_cells)
        recv_phase = steer_angle(recv_x, recv_y, vox_x, vox_y, vox_z, frequency, gate_len)
        rx_cosine = jnp.cos(recv_phase).astype(jnp.bfloat16)
        rx_sine = jnp.sin(recv_phase).astype(jnp.bfloat16)
        steer_rx = jnp.concatenate(
            [
                jnp.concatenate([rx_cosine, rx_sine], axis=2),
                jnp.concatenate([-rx_sine, rx_cosine], axis=2),
            ],
            axis=1,
        )
        products = jnp.einsum(
            "ftl,flv->ftv", left_side, steer_rx, preferred_element_type=jnp.float32
        )
        prod_real = products[:, :, :block_width]
        prod_imag = products[:, :, block_width:]
        send_phase = steer_angle(send_x, send_y, vox_x, vox_y, vox_z, frequency, gate_len)
        tx_cosine = jnp.cos(send_phase)
        tx_sine = jnp.sin(send_phase)
        image_real = jnp.sum(prod_real * tx_cosine - prod_imag * tx_sine, axis=(0, 1))
        image_imag = jnp.sum(prod_real * tx_sine + prod_imag * tx_cosine, axis=(0, 1))
        return jnp.stack([image_real, image_imag])

    blocks = lax.map(image_block, voxel_blocks)
    partial_value = blocks.transpose(1, 0, 2).reshape(2, voxel_count) * (
        1.0 / (elements * math.sqrt(BINS))
    )
    image_part = lax.psum_scatter(partial_value, ("tx", "rx"), scatter_dimension=1, tiled=True)
    return image_part


def cosine_fit():
    grid = np.cos(np.pi * (np.arange(400) + 0.5) / 400) * 0.125 + 0.125
    fit = np.polynomial.chebyshev.Chebyshev.fit(
        grid, np.cos(2.0 * np.pi * np.sqrt(grid)), 8, domain=[0.0, 0.25]
    )
    return [float(c) for c in fit.convert(kind=np.polynomial.Polynomial).coef]


COSINE = cosine_fit()


def cos_turns(turns):
    rest = turns - jnp.floor(turns + 0.5)
    square = rest * rest
    total = jnp.full_like(square, COSINE[-1])
    for factor in COSINE[-2::-1]:
        total = total * square + factor
    return total


def iota(shape, axis):
    return lax.broadcasted_iota(jnp.int32, shape, axis)


def one_hot(mask):
    return jnp.where(mask, 1.0, 0.0).astype(jnp.bfloat16)


def matmul(left, right):
    return jnp.dot(left, right, preferred_element_type=jnp.float32)


def filter_lanes(taps, gate_len):
    first_bin = gate_len // 12

    def turns(rows):
        lane = iota((rows, LANES), 1)
        step = iota((rows, LANES), 0) * (first_bin + (lane & (BINS - 1)))
        return (step & (gate_len - 1)).astype(jnp.float32) * (1.0 / gate_len), lane

    tap_turns, _ = turns(taps)
    tables = jnp.concatenate([cos_turns(tap_turns), cos_turns(tap_turns - 0.25)], axis=1)
    high = tables.astype(jnp.bfloat16)
    rest = tables - high.astype(jnp.float32)
    middle = rest.astype(jnp.bfloat16)
    low = (rest - middle.astype(jnp.float32)).astype(jnp.bfloat16)
    reached = iota((gate_len, taps), 1) <= iota((gate_len, taps), 0)
    gate_turns, lane = turns(gate_len)
    gate_turns = gate_turns + jnp.where((lane & BINS) != 0, 0.25, 0.0)
    scale = 1.0 / math.sqrt(taps * gate_len)
    by_cosine = cos_turns(gate_turns) * scale
    by_sine = cos_turns(gate_turns - 0.25) * scale

    def table(excitation):
        weight = jnp.where(reached, excitation.astype(jnp.float32), 0.0).astype(jnp.bfloat16)
        sums = matmul(weight, high) + (matmul(weight, middle) + matmul(weight, low))
        return (by_cosine * sums[:, :LANES] + by_sine * sums[:, LANES:]).astype(jnp.bfloat16)

    return table


def steer_rows(elem_x, elem_y, points, gate_len, quarter, store):
    middle = gate_len // 12 + BINS // 2
    distance = jnp.sqrt(
        (elem_x - points[0]) ** 2 + (elem_y - points[1]) ** 2 + points[2] ** 2
    )
    turns = distance * (samples_per_mm / gate_len)
    twice = 2.0 * cos_turns(turns)
    for kind in range(2):
        back = 0.25 * kind
        now = cos_turns(turns * middle - back)
        before = cos_turns(turns * (middle - 1) - back)
        store(kind, BINS // 2, now)
        store(kind, BINS // 2 - 1, before)
        low, high = before, now
        for f in range(BINS // 2 - 2, -1, -1):
            low, high = twice * low - high, low
            store(kind, f, low)
        low, high = before, now
        for f in range(BINS // 2 + 1, BINS):
            low, high = high, twice * high - low
            store(kind, f, high)


def kernel(
    tx_count,
    rx_count,
    cap_any,
    grid_any,
    exc_any,
    vox_any,
    out_ref,
    cap,
    grid,
    exc,
    vox,
    steer_rx,
    steer_tx,
    send_spec,
    recv_spec,
    send_part,
    recv_part,
    load_sems,
    spec_sems,
    part_sems,
):
    devices = tx_count * rx_count
    tx_rows, rx_cols, gate_len = cap.shape
    subrun = rx_cols // tx_count
    channels = 2 * BINS
    width = subrun * subrun * channels
    voxel_count = vox.shape[1]
    owned = voxel_count // devices
    me_tx, me_rx = lax.axis_index("tx"), lax.axis_index("rx")
    me = me_tx * rx_count + me_rx
    slot = me_rx * tx_count + me_tx

    loads = [
        pltpu.make_async_copy(source, target, load_sems.at[i])
        for i, (source, target) in enumerate(
            ((exc_any, exc), (cap_any, cap), (grid_any, grid), (vox_any, vox))
        )
    ]
    for load in loads:
        load.start()

    def place(other):
        return lax.div(other, rx_count), lax.rem(other, rx_count)

    def wait_rows(ref, semaphore, count):
        for rows in range(1, devices):

            @pl.when(count == rows)
            def _(rows=rows):
                some = ref.at[pl.ds(0, rows)]
                pltpu.make_async_copy(some, some, semaphore).wait()

    barrier = pltpu.get_barrier_semaphore()

    @pl.loop(me + 1, devices)
    def _(other):
        pl.semaphore_signal(
            barrier, inc=1, device_id=place(other), device_id_type=pl.DeviceIdType.MESH
        )

    make_table = filter_lanes(exc.shape[1], gate_len)
    group = iota((rx_cols, width), 1) // channels
    inner = iota((rx_cols, width), 0) & (subrun - 1)
    own_key = group - inner
    sent_key = group - subrun * inner
    pairs = tx_rows * rx_cols
    pair = iota((devices, pairs), 1)
    partner_row = (pair // (rx_cols * subrun)) * tx_count + (pair & (rx_cols - 1)) // subrun
    gather = one_hot(partner_row == iota((devices, pairs), 0))
    loads[0].wait()
    table = make_table(exc[...])
    table = jnp.concatenate([table] * (width // LANES), axis=1)
    loads[1].wait()
    rows = []
    for t in range(tx_rows):
        spec = matmul(cap[t], table)
        own = jnp.where(own_key == subrun * (t % subrun), spec, 0.0)
        sent = jnp.where(sent_key == t % subrun, spec, 0.0)
        rows.append(jnp.concatenate([own, sent], axis=1).astype(jnp.bfloat16))
    rows = jnp.concatenate(rows, axis=0)
    both = matmul(gather, rows)
    own_spec = both[:, :width]
    send_spec[...] = both[:, width:].reshape(devices, 1, width)
    recv_spec[pl.ds(slot, 1)] = send_spec[pl.ds(slot, 1)]

    @pl.when(me > 0)
    def _():
        pl.semaphore_wait(barrier, me)

    @pl.loop(0, me)
    def _(other):
        tx, rx = place(other)
        pltpu.make_async_remote_copy(
            src_ref=send_spec.at[rx * tx_count + tx],
            dst_ref=recv_spec.at[slot],
            send_sem=spec_sems.at[0],
            recv_sem=spec_sems.at[1],
            device_id=(tx, rx),
            device_id_type=pl.DeviceIdType.MESH,
        ).start()

    loads[2].wait()
    loads[3].wait()
    elements = grid.shape[1]
    cells = grid[...].astype(jnp.float32)
    x_line = (cells[0:1] - 0.5 * (elements // 32 - 1)) * pitch_mm
    y_line = (cells[1:2] - 15.5) * pitch_mm
    points = voxel_points(vox[...])
    points = tuple(p.reshape(1, voxel_count) for p in points)

    def columns(chosen):
        return (
            jnp.sum(jnp.where(chosen, x_line, 0.0), axis=1, keepdims=True),
            jnp.sum(jnp.where(chosen, y_line, 0.0), axis=1, keepdims=True),
        )

    chunk = 16
    for first in range(0, rx_cols, chunk):
        j = iota((chunk, elements), 0) + first
        element = (j // subrun) * tx_rows + me_rx * subrun + (j & (subrun - 1))
        elem_x, elem_y = columns(iota((chunk, elements), 1) == element)

        def store(kind, f, values, first=first):
            steer_rx[f, pl.ds(kind * rx_cols + first, chunk), :] = values.astype(jnp.bfloat16)

        steer_rows(elem_x, elem_y, points, gate_len, 0, store)
    element = iota((tx_rows, elements), 0) + me_tx * tx_rows
    elem_x, elem_y = columns(iota((tx_rows, elements), 1) == element)

    def store_tx(kind, f, values):
        steer_tx[f, pl.ds(kind * tx_rows, tx_rows), :] = values

    steer_rows(elem_x, elem_y, points, gate_len, 0, store_tx)

    same = one_hot(iota((width, width), 0) // channels == iota((width, width), 1) // channels)
    spread_rows = 2 * rx_cols
    spread = one_hot(
        iota((spread_rows, 2 * tx_count), 0) // subrun == iota((spread_rows, 2 * tx_count), 1)
    )
    long = rx_count * width
    kept = (iota((spread_rows, long), 1) // channels) % subrun == (
        iota((spread_rows, long), 0) & (subrun - 1)
    )
    fold_row = iota((channels * tx_rows, long), 0)
    fold_lane = iota((channels * tx_rows, long), 1)
    fold = one_hot(
        ((fold_row & (tx_rows - 1)) == fold_lane // (subrun * channels))
        & (fold_row // tx_rows == (fold_lane & (BINS - 1)) * 2 + ((fold_lane // BINS) & 1))
    )

    row = iota((devices, width), 0)
    sender = lax.rem(row, tx_count) * rx_count + lax.div(row, tx_count)
    times = jnp.where(sender > me, 2.0, 1.0)
    used = sender >= me
    imag_lane = (iota((devices, width), 1) & BINS) != 0

    wait_rows(recv_spec, spec_sems.at[1], devices - 1 - me)
    averaged = jnp.where(used, own_spec + recv_spec[...].reshape(devices, width), 0.0) * 0.5
    square = averaged * averaged
    high = square.astype(jnp.bfloat16)
    low = (square - high.astype(jnp.float32)).astype(jnp.bfloat16)
    power = (matmul(high, same) + matmul(low, same)) * (1.0 / channels)
    whitened = averaged * lax.rsqrt(jnp.maximum(power, power_floor)) * times
    turned = jnp.where(
        imag_lane, pltpu.roll(whitened, BINS, 1), -pltpu.roll(whitened, width - BINS, 1)
    )

    def side(values):
        return jnp.concatenate(
            [values[b * tx_count : (b + 1) * tx_count] for b in range(rx_count)], axis=1
        )

    both = jnp.concatenate([side(whitened), side(turned)], axis=0).astype(jnp.bfloat16)
    wide = jnp.where(kept, matmul(spread, both), 0.0).astype(jnp.bfloat16)
    left = lax.dot_general(
        fold, wide, (((1,), (1,)), ((), ())), preferred_element_type=jnp.float32
    ).astype(jnp.bfloat16)
    real = jnp.zeros((tx_rows, voxel_count), jnp.float32)
    imag = jnp.zeros((tx_rows, voxel_count), jnp.float32)
    for f in range(BINS):
        products = matmul(left[2 * tx_rows * f : 2 * tx_rows * (f + 1)], steer_rx[f])
        prod_real, prod_imag = products[:tx_rows], products[tx_rows:]
        tx_cosine, tx_sine = steer_tx[f, :tx_rows, :], steer_tx[f, tx_rows:, :]
        real += prod_real * tx_cosine - prod_imag * tx_sine
        imag += prod_real * tx_sine + prod_imag * tx_cosine
    image = jnp.concatenate(
        [jnp.sum(real, axis=0, keepdims=True), jnp.sum(imag, axis=0, keepdims=True)], axis=0
    ) * (1.0 / (elements * math.sqrt(BINS)))
    for tile in range(voxel_count // LANES):
        send_part[tile] = image[:, tile * LANES : (tile + 1) * LANES]
    per_tile = LANES // owned

    @pl.loop(0, devices - 1)
    def _(i):
        other = i + jnp.where(i >= me, 1, 0)
        tx, rx = place(other)
        pltpu.make_async_remote_copy(
            src_ref=send_part.at[lax.div(other, per_tile)],
            dst_ref=recv_part.at[me],
            send_sem=part_sems.at[0],
            recv_sem=part_sems.at[1],
            device_id=(tx, rx),
            device_id_type=pl.DeviceIdType.MESH,
        ).start()

    recv_part[pl.ds(me, 1)] = send_part[pl.ds(lax.div(me, per_tile), 1)]
    all_but_one = recv_part.at[pl.ds(0, devices - 1)]
    pltpu.make_async_copy(all_but_one, all_but_one, part_sems.at[1]).wait()
    total = jnp.sum(recv_part[...], axis=0)
    shift = lax.rem(LANES - owned * lax.rem(me, per_tile), LANES)
    out_ref[...] = pltpu.roll(total, shift, 1)[:, :owned]
    wait_rows(send_spec, spec_sems.at[0], me)
    pltpu.make_async_copy(all_but_one, all_but_one, part_sems.at[0]).wait()


def small(captures, elem_grid, excitation, voxels):
    tx_count = lax.axis_size("tx")
    rx_count = lax.axis_size("rx")
    devices = tx_count * rx_count
    tx_rows, rx_cols, gate_len = captures.shape
    voxel_count = voxels.shape[1]
    width = (rx_cols // tx_count) ** 2 * 2 * BINS
    excitation = excitation.reshape(1, -1)
    operands = [
        pltpu.with_memory_space_constraint(x, pltpu.HBM)
        for x in (captures, elem_grid, excitation, voxels)
    ]
    return pl.pallas_call(
        functools.partial(kernel, tx_count, rx_count),
        out_shape=pltpu.VMEM((2, voxel_count // devices), jnp.float32),
        in_specs=[pl.BlockSpec(memory_space=pltpu.HBM)] * 4,
        out_specs=pl.BlockSpec(memory_space=pltpu.VMEM),
        scratch_shapes=[
            pltpu.VMEM(captures.shape, captures.dtype),
            pltpu.VMEM(elem_grid.shape, jnp.int32),
            pltpu.VMEM(excitation.shape, jnp.int32),
            pltpu.VMEM(voxels.shape, jnp.int32),
            pltpu.VMEM((BINS, 2 * rx_cols, voxel_count), jnp.bfloat16),
            pltpu.VMEM((BINS, 2 * tx_rows, voxel_count), jnp.float32),
            pltpu.VMEM((devices, 1, width), jnp.float32),
            pltpu.VMEM((devices, 1, width), jnp.float32),
            pltpu.VMEM((voxel_count // LANES, 2, LANES), jnp.float32),
            pltpu.VMEM((devices, 2, LANES), jnp.float32),
            pltpu.SemaphoreType.DMA((4,)),
            pltpu.SemaphoreType.DMA((2,)),
            pltpu.SemaphoreType.DMA((2,)),
        ],
        compiler_params=pltpu.CompilerParams(
            collective_id=0, has_side_effects=True, vmem_limit_bytes=32 * 1024 * 1024
        ),
    )(*operands)


def local(captures, elem_grid, excitation, voxels):
    tx_count = lax.axis_size("tx")
    devices = tx_count * lax.axis_size("rx")
    tx_rows, rx_cols, _ = captures.shape
    fits = (
        tx_rows == 8
        and rx_cols == 64
        and rx_cols // tx_count == 4
        and voxels.shape[1] <= 1024
        and LANES % (voxels.shape[1] // devices) == 0
    )
    return (small if fits else general)(captures, elem_grid, excitation, voxels)


def solution(mesh):
    placed = (P("tx", "rx", None), P(), P(), P())
    return jax.shard_map(
        local, mesh=mesh, in_specs=placed, out_specs=P(None, ("tx", "rx")), check_vma=False
    )
```

```python
import functools
import math

import jax
import jax.numpy as jnp
import numpy as np
from jax import lax
from jax.experimental import pallas as pl
from jax.experimental.pallas import tpu as pltpu
from jax.sharding import PartitionSpec as P

BINS = 8
LANES = 128


samples_per_mm = 8.4746
pitch_mm = 0.5
power_floor = 0.1


def filter_table(excitation, gate_len, bin_count):
    tap_count = excitation.shape[0]
    first_bin = gate_len // 12
    lag_index = (
        jnp.arange(gate_len, dtype=jnp.int32)[:, None]
        - jnp.arange(tap_count, dtype=jnp.int32)[None, :]
    )
    frequency = first_bin + jnp.arange(bin_count, dtype=jnp.int32)
    phase_turns = jnp.mod(lag_index[:, :, None] * frequency[None, None, :], gate_len)
    phases = 2.0 * math.pi / gate_len * phase_turns.astype(jnp.float32)
    weight = jnp.where(lag_index >= 0, excitation[None, :], 0).astype(jnp.float32)[:, :, None]
    norm_scale = 1.0 / math.sqrt(tap_count * gate_len)
    real_part = jnp.sum(weight * jnp.cos(phases), axis=1) * norm_scale
    imag_part = -jnp.sum(weight * jnp.sin(phases), axis=1) * norm_scale
    return jnp.concatenate([real_part, imag_part], axis=1).astype(jnp.bfloat16)


def element_points(grid_cells, grid_rows):
    elem_x = (grid_cells[0].astype(jnp.float32) - 0.5 * (grid_rows - 1)) * pitch_mm
    elem_y = (grid_cells[1].astype(jnp.float32) - 15.5) * pitch_mm
    return (elem_x, elem_y)


def voxel_points(block_cells):
    cells_float = block_cells.astype(jnp.float32)
    return (
        (cells_float[0] - 31.5) * 0.5,
        (cells_float[1] - 31.5) * 0.5,
        10.0 + cells_float[2] * 0.5,
    )


def steer_angle(elem_x, elem_y, vox_x, vox_y, vox_z, frequency, gate_len):
    distance = jnp.sqrt(
        (elem_x[:, None] - vox_x[None, :]) ** 2
        + (elem_y[:, None] - vox_y[None, :]) ** 2
        + vox_z[None, :] ** 2
    )
    delay = distance * (samples_per_mm / gate_len)
    return 2.0 * math.pi * frequency.astype(jnp.float32)[:, None, None] * delay[None]


def general(captures, elem_grid, excitation, voxels):
    tx_count = lax.axis_size("tx")
    rx_count = lax.axis_size("rx")
    tx_rows, rx_cols, gate_len = captures.shape
    subrun = rx_cols // tx_count
    channels = 2 * BINS
    elements = tx_rows * tx_count
    matched = filter_table(excitation, gate_len, BINS)
    pieces = captures.reshape(rx_count, subrun, tx_count, subrun, gate_len)
    local_spec = jnp.einsum(
        "bhaxs,sc->cbhax", pieces, matched, preferred_element_type=jnp.float32
    ).astype(jnp.bfloat16)
    arrived = lax.all_to_all(
        lax.all_to_all(pieces, "tx", split_axis=2, concat_axis=2, tiled=True),
        "rx",
        split_axis=0,
        concat_axis=0,
        tiled=True,
    )
    mirror = jnp.einsum(
        "bhgxs,sc->cbxgh", arrived, matched, preferred_element_type=jnp.float32
    ).astype(jnp.bfloat16)
    averaged = ((local_spec.astype(jnp.float32) + mirror.astype(jnp.float32)) * 0.5).reshape(
        channels, tx_rows, rx_cols
    )
    power = jnp.mean(averaged * averaged, axis=0, keepdims=True)
    whitened = (
        (averaged / jnp.sqrt(jnp.maximum(power, power_floor)))
        .astype(jnp.bfloat16)
        .reshape(2, BINS, tx_rows, rx_cols)
    )
    left_side = jnp.concatenate([whitened[0], whitened[1]], axis=2)
    tx_cells = lax.dynamic_slice_in_dim(elem_grid, lax.axis_index("tx") * tx_rows, tx_rows, axis=1)
    rx_cells = lax.dynamic_index_in_dim(
        elem_grid.reshape(2, tx_count, rx_count, subrun),
        lax.axis_index("rx"),
        axis=2,
        keepdims=False,
    ).reshape(2, rx_cols)
    send_x, send_y = element_points(tx_cells, elements // 32)
    recv_x, recv_y = element_points(rx_cells, elements // 32)
    frequency = gate_len // 12 + jnp.arange(BINS, dtype=jnp.int32)
    voxel_count = voxels.shape[1]
    block_width = min(512, voxel_count)
    voxel_blocks = voxels.reshape(3, voxel_count // block_width, block_width).transpose(1, 0, 2)

    def image_block(block_cells):
        vox_x, vox_y, vox_z = voxel_points(block_cells)
        recv_phase = steer_angle(recv_x, recv_y, vox_x, vox_y, vox_z, frequency, gate_len)
        rx_cosine = jnp.cos(recv_phase).astype(jnp.bfloat16)
        rx_sine = jnp.sin(recv_phase).astype(jnp.bfloat16)
        steer_rx = jnp.concatenate(
            [
                jnp.concatenate([rx_cosine, rx_sine], axis=2),
                jnp.concatenate([-rx_sine, rx_cosine], axis=2),
            ],
            axis=1,
        )
        products = jnp.einsum(
            "ftl,flv->ftv", left_side, steer_rx, preferred_element_type=jnp.float32
        )
        prod_real = products[:, :, :block_width]
        prod_imag = products[:, :, block_width:]
        send_phase = steer_angle(send_x, send_y, vox_x, vox_y, vox_z, frequency, gate_len)
        tx_cosine = jnp.cos(send_phase)
        tx_sine = jnp.sin(send_phase)
        image_real = jnp.sum(prod_real * tx_cosine - prod_imag * tx_sine, axis=(0, 1))
        image_imag = jnp.sum(prod_real * tx_sine + prod_imag * tx_cosine, axis=(0, 1))
        return jnp.stack([image_real, image_imag])

    blocks = lax.map(image_block, voxel_blocks)
    partial_value = blocks.transpose(1, 0, 2).reshape(2, voxel_count) * (
        1.0 / (elements * math.sqrt(BINS))
    )
    image_part = lax.psum_scatter(partial_value, ("tx", "rx"), scatter_dimension=1, tiled=True)
    return image_part


def cosine_fit():
    grid = np.cos(np.pi * (np.arange(400) + 0.5) / 400) * 0.125 + 0.125
    fit = np.polynomial.chebyshev.Chebyshev.fit(
        grid, np.cos(2.0 * np.pi * np.sqrt(grid)), 8, domain=[0.0, 0.25]
    )
    return [float(c) for c in fit.convert(kind=np.polynomial.Polynomial).coef]


COSINE = cosine_fit()


def cos_turns(turns):
    rest = turns - jnp.floor(turns + 0.5)
    square = rest * rest
    total = jnp.full_like(square, COSINE[-1])
    for factor in COSINE[-2::-1]:
        total = total * square + factor
    return total


def iota(shape, axis):
    return lax.broadcasted_iota(jnp.int32, shape, axis)


def one_hot(mask):
    return jnp.where(mask, 1.0, 0.0).astype(jnp.bfloat16)


def matmul(left, right):
    return jnp.dot(left, right, preferred_element_type=jnp.float32)


def filter_lanes(taps, gate_len):
    first_bin = gate_len // 12

    def turns(rows):
        lane = iota((rows, LANES), 1)
        step = iota((rows, LANES), 0) * (first_bin + (lane & (BINS - 1)))
        return (step & (gate_len - 1)).astype(jnp.float32) * (1.0 / gate_len), lane

    tap_turns, _ = turns(taps)
    tables = jnp.concatenate([cos_turns(tap_turns), cos_turns(tap_turns - 0.25)], axis=1)
    high = tables.astype(jnp.bfloat16)
    rest = tables - high.astype(jnp.float32)
    middle = rest.astype(jnp.bfloat16)
    low = (rest - middle.astype(jnp.float32)).astype(jnp.bfloat16)
    reached = iota((gate_len, taps), 1) <= iota((gate_len, taps), 0)
    gate_turns, lane = turns(gate_len)
    gate_turns = gate_turns + jnp.where((lane & BINS) != 0, 0.25, 0.0)
    scale = 1.0 / math.sqrt(taps * gate_len)
    by_cosine = cos_turns(gate_turns) * scale
    by_sine = cos_turns(gate_turns - 0.25) * scale

    def table(excitation):
        weight = jnp.where(reached, excitation.astype(jnp.float32), 0.0).astype(jnp.bfloat16)
        sums = matmul(weight, high) + (matmul(weight, middle) + matmul(weight, low))
        return (by_cosine * sums[:, :LANES] + by_sine * sums[:, LANES:]).astype(jnp.bfloat16)

    return table


def steer_rows(elem_x, elem_y, points, gate_len, quarter, store):
    middle = gate_len // 12 + BINS // 2
    distance = jnp.sqrt(
        (elem_x - points[0]) ** 2 + (elem_y - points[1]) ** 2 + points[2] ** 2
    )
    turns = distance * (samples_per_mm / gate_len)
    twice = 2.0 * cos_turns(turns)
    for kind in range(2):
        back = 0.25 * kind
        now = cos_turns(turns * middle - back)
        before = cos_turns(turns * (middle - 1) - back)
        store(kind, BINS // 2, now)
        store(kind, BINS // 2 - 1, before)
        low, high = before, now
        for f in range(BINS // 2 - 2, -1, -1):
            low, high = twice * low - high, low
            store(kind, f, low)
        low, high = before, now
        for f in range(BINS // 2 + 1, BINS):
            low, high = high, twice * high - low
            store(kind, f, high)


def kernel(
    tx_count,
    rx_count,
    cap_any,
    grid_any,
    exc_any,
    vox_any,
    out_ref,
    cap,
    grid,
    exc,
    vox,
    steer_rx,
    steer_tx,
    send_spec,
    recv_spec,
    send_part,
    recv_part,
    load_sems,
    spec_sems,
    part_sems,
):
    devices = tx_count * rx_count
    tx_rows, rx_cols, gate_len = cap.shape
    subrun = rx_cols // tx_count
    channels = 2 * BINS
    width = subrun * subrun * channels
    voxel_count = vox.shape[1]
    owned = voxel_count // devices
    me_tx, me_rx = lax.axis_index("tx"), lax.axis_index("rx")
    me = me_tx * rx_count + me_rx
    slot = me_rx * tx_count + me_tx

    halves = [pl.ds(b * subrun, subrun) for b in range(rx_count)]
    pieces = [(cap_any.at[half], cap.at[half]) for half in halves]
    pieces += [(exc_any, exc), (grid_any, grid), (vox_any, vox)]
    loads = [
        pltpu.make_async_copy(source, target, load_sems.at[i])
        for i, (source, target) in enumerate(pieces)
    ]
    for load in loads:
        load.start()

    def place(other):
        return lax.div(other, rx_count), lax.rem(other, rx_count)

    def wait_rows(ref, semaphore, count, low=0, high=devices):
        if high - low > 1:
            middle = (low + high) // 2
            for side, span in ((count < middle, (low, middle)), (count >= middle, (middle, high))):

                @pl.when(side)
                def _(span=span):
                    wait_rows(ref, semaphore, count, *span)
        elif low:
            some = ref.at[pl.ds(0, low)]
            pltpu.make_async_copy(some, some, semaphore).wait()

    barrier = pltpu.get_barrier_semaphore()

    @pl.loop(me + 1, devices)
    def _(other):
        pl.semaphore_signal(
            barrier, inc=1, device_id=place(other), device_id_type=pl.DeviceIdType.MESH
        )

    make_table = filter_lanes(exc.shape[1], gate_len)
    pairs = subrun * rx_cols
    group = iota((pairs, width), 1) // channels
    outer = iota((pairs, width), 0) // rx_cols
    inner = iota((pairs, width), 0) & (subrun - 1)
    own_kept = group == subrun * outer + inner
    sent_kept = group == subrun * inner + outer
    pair = iota((tx_count, pairs), 1)
    gather = one_hot((pair & (rx_cols - 1)) // subrun == iota((tx_count, pairs), 0))
    loads[rx_count].wait()
    table = make_table(exc[...])
    table = jnp.concatenate([table] * (width // LANES), axis=1)
    own_spec = []
    for b in range(rx_count):
        loads[b].wait()
        spec = matmul(cap[halves[b]].reshape(pairs, gate_len), table)
        kept = [jnp.where(mask, spec, 0.0) for mask in (own_kept, sent_kept)]
        both = matmul(gather, jnp.concatenate(kept, axis=1).astype(jnp.bfloat16))
        own_spec.append(both[:, :width])
        send_spec[pl.ds(b * tx_count, tx_count)] = both[:, width:].reshape(tx_count, 1, width)
    own_spec = jnp.concatenate(own_spec, axis=0)
    recv_spec[pl.ds(slot, 1)] = send_spec[pl.ds(slot, 1)]

    @pl.when(me > 0)
    def _():
        pl.semaphore_wait(barrier, me)

    @pl.loop(0, me)
    def _(other):
        tx, rx = place(other)
        pltpu.make_async_remote_copy(
            src_ref=send_spec.at[rx * tx_count + tx],
            dst_ref=recv_spec.at[slot],
            send_sem=spec_sems.at[0],
            recv_sem=spec_sems.at[1],
            device_id=(tx, rx),
            device_id_type=pl.DeviceIdType.MESH,
        ).start()

    loads[rx_count + 1].wait()
    loads[rx_count + 2].wait()
    elements = grid.shape[1]
    cells = grid[...].astype(jnp.float32)
    x_line = (cells[0:1] - 0.5 * (elements // 32 - 1)) * pitch_mm
    y_line = (cells[1:2] - 15.5) * pitch_mm
    points = voxel_points(vox[...])
    points = tuple(p.reshape(1, voxel_count) for p in points)

    def columns(chosen):
        return (
            jnp.sum(jnp.where(chosen, x_line, 0.0), axis=1, keepdims=True),
            jnp.sum(jnp.where(chosen, y_line, 0.0), axis=1, keepdims=True),
        )

    chunk = 16
    for first in range(0, rx_cols, chunk):
        j = iota((chunk, elements), 0) + first
        element = (j // subrun) * tx_rows + me_rx * subrun + (j & (subrun - 1))
        elem_x, elem_y = columns(iota((chunk, elements), 1) == element)

        def store(kind, f, values, first=first):
            steer_rx[f, pl.ds(kind * rx_cols + first, chunk), :] = values.astype(jnp.bfloat16)

        steer_rows(elem_x, elem_y, points, gate_len, 0, store)
    element = iota((tx_rows, elements), 0) + me_tx * tx_rows
    elem_x, elem_y = columns(iota((tx_rows, elements), 1) == element)

    def store_tx(kind, f, values):
        steer_tx[f, pl.ds(kind * tx_rows, tx_rows), :] = values

    steer_rows(elem_x, elem_y, points, gate_len, 0, store_tx)

    same = one_hot(iota((width, width), 0) // channels == iota((width, width), 1) // channels)
    spread_rows = 2 * rx_cols
    spread = one_hot(
        iota((spread_rows, 2 * tx_count), 0) // subrun == iota((spread_rows, 2 * tx_count), 1)
    )
    long = rx_count * width
    kept = (iota((spread_rows, long), 1) // channels) % subrun == (
        iota((spread_rows, long), 0) & (subrun - 1)
    )
    fold_row = iota((channels * tx_rows, long), 0)
    fold_lane = iota((channels * tx_rows, long), 1)
    fold = one_hot(
        ((fold_row & (tx_rows - 1)) == fold_lane // (subrun * channels))
        & (fold_row // tx_rows == (fold_lane & (BINS - 1)) * 2 + ((fold_lane // BINS) & 1))
    )

    row = iota((devices, width), 0)
    sender = lax.rem(row, tx_count) * rx_count + lax.div(row, tx_count)
    times = jnp.where(sender > me, 2.0, 1.0)
    used = sender >= me
    imag_lane = (iota((devices, width), 1) & BINS) != 0

    wait_rows(recv_spec, spec_sems.at[1], devices - 1 - me)
    averaged = jnp.where(used, own_spec + recv_spec[...].reshape(devices, width), 0.0) * 0.5
    square = averaged * averaged
    high = square.astype(jnp.bfloat16)
    low = (square - high.astype(jnp.float32)).astype(jnp.bfloat16)
    power = (matmul(high, same) + matmul(low, same)) * (1.0 / channels)
    whitened = averaged * lax.rsqrt(jnp.maximum(power, power_floor)) * times
    turned = jnp.where(
        imag_lane, pltpu.roll(whitened, BINS, 1), -pltpu.roll(whitened, width - BINS, 1)
    )

    def side(values):
        return jnp.concatenate(
            [values[b * tx_count : (b + 1) * tx_count] for b in range(rx_count)], axis=1
        )

    both = jnp.concatenate([side(whitened), side(turned)], axis=0).astype(jnp.bfloat16)
    wide = jnp.where(kept, matmul(spread, both), 0.0).astype(jnp.bfloat16)
    left = lax.dot_general(
        fold, wide, (((1,), (1,)), ((), ())), preferred_element_type=jnp.float32
    ).astype(jnp.bfloat16)
    per_tile = LANES // owned
    scale = 1.0 / (elements * math.sqrt(BINS))
    tiles = voxel_count // LANES
    for first, last in ((0, 1), (1, tiles)):
        lanes = pl.ds(first * LANES, (last - first) * LANES)
        real = jnp.zeros((tx_rows, (last - first) * LANES), jnp.float32)
        imag = jnp.zeros_like(real)
        for f in range(BINS):
            products = matmul(
                left[2 * tx_rows * f : 2 * tx_rows * (f + 1)], steer_rx[f, :, lanes]
            )
            prod_real, prod_imag = products[:tx_rows], products[tx_rows:]
            tx_cosine = steer_tx[f, pl.ds(0, tx_rows), lanes]
            tx_sine = steer_tx[f, pl.ds(tx_rows, tx_rows), lanes]
            real += prod_real * tx_cosine - prod_imag * tx_sine
            imag += prod_real * tx_sine + prod_imag * tx_cosine
        image = jnp.concatenate(
            [jnp.sum(real, axis=0, keepdims=True), jnp.sum(imag, axis=0, keepdims=True)], axis=0
        )
        image = image * scale
        for tile in range(first, last):
            begin = (tile - first) * LANES
            send_part[tile] = image[:, begin : begin + LANES]

        @pl.loop(first * per_tile, last * per_tile)
        def _(other):
            @pl.when(other != me)
            def _():
                pltpu.make_async_remote_copy(
                    src_ref=send_part.at[lax.div(other, per_tile)],
                    dst_ref=recv_part.at[me],
                    send_sem=part_sems.at[0],
                    recv_sem=part_sems.at[1],
                    device_id=place(other),
                    device_id_type=pl.DeviceIdType.MESH,
                ).start()

    recv_part[pl.ds(me, 1)] = send_part[pl.ds(lax.div(me, per_tile), 1)]
    all_but_one = recv_part.at[pl.ds(0, devices - 1)]
    wait_rows(send_spec, spec_sems.at[0], me)
    for semaphore in range(2):
        pltpu.make_async_copy(all_but_one, all_but_one, part_sems.at[semaphore]).wait()
    total = jnp.sum(recv_part[...], axis=0)
    shift = lax.rem(LANES - owned * lax.rem(me, per_tile), LANES)
    out_ref[...] = pltpu.roll(total, shift, 1)[:, :owned]


def small(captures, elem_grid, excitation, voxels):
    tx_count = lax.axis_size("tx")
    rx_count = lax.axis_size("rx")
    devices = tx_count * rx_count
    tx_rows, rx_cols, gate_len = captures.shape
    voxel_count = voxels.shape[1]
    width = (rx_cols // tx_count) ** 2 * 2 * BINS
    excitation = excitation.reshape(1, -1)
    operands = [
        pltpu.with_memory_space_constraint(x, pltpu.HBM)
        for x in (captures, elem_grid, excitation, voxels)
    ]
    return pl.pallas_call(
        functools.partial(kernel, tx_count, rx_count),
        out_shape=pltpu.VMEM((2, voxel_count // devices), jnp.float32),
        in_specs=[pl.BlockSpec(memory_space=pltpu.HBM)] * 4,
        out_specs=pl.BlockSpec(memory_space=pltpu.VMEM),
        scratch_shapes=[
            pltpu.VMEM(captures.shape, captures.dtype),
            pltpu.VMEM(elem_grid.shape, jnp.int32),
            pltpu.VMEM(excitation.shape, jnp.int32),
            pltpu.VMEM(voxels.shape, jnp.int32),
            pltpu.VMEM((BINS, 2 * rx_cols, voxel_count), jnp.bfloat16),
            pltpu.VMEM((BINS, 2 * tx_rows, voxel_count), jnp.float32),
            pltpu.VMEM((devices, 1, width), jnp.float32),
            pltpu.VMEM((devices, 1, width), jnp.float32),
            pltpu.VMEM((voxel_count // LANES, 2, LANES), jnp.float32),
            pltpu.VMEM((devices, 2, LANES), jnp.float32),
            pltpu.SemaphoreType.DMA((rx_count + 3,)),
            pltpu.SemaphoreType.DMA((2,)),
            pltpu.SemaphoreType.DMA((2,)),
        ],
        compiler_params=pltpu.CompilerParams(
            collective_id=0, has_side_effects=True, vmem_limit_bytes=32 * 1024 * 1024
        ),
    )(*operands)


def local(captures, elem_grid, excitation, voxels):
    tx_count = lax.axis_size("tx")
    devices = tx_count * lax.axis_size("rx")
    tx_rows, rx_cols, _ = captures.shape
    fits = (
        tx_rows == 8
        and rx_cols == 64
        and rx_cols // tx_count == 4
        and voxels.shape[1] <= 1024
        and LANES % (voxels.shape[1] // devices) == 0
    )
    return (small if fits else general)(captures, elem_grid, excitation, voxels)


def solution(mesh):
    placed = (P("tx", "rx", None), P(), P(), P())
    return jax.shard_map(
        local, mesh=mesh, in_specs=placed, out_specs=P(None, ("tx", "rx")), check_vma=False
    )
```

```python
import functools
import math

import jax
import jax.numpy as jnp
import numpy as np
from jax import lax
from jax.experimental import pallas as pl
from jax.experimental.pallas import tpu as pltpu
from jax.sharding import PartitionSpec as P

BINS = 8
LANES = 128


samples_per_mm = 8.4746
pitch_mm = 0.5
power_floor = 0.1


def filter_table(excitation, gate_len, bin_count):
    tap_count = excitation.shape[0]
    first_bin = gate_len // 12
    lag_index = (
        jnp.arange(gate_len, dtype=jnp.int32)[:, None]
        - jnp.arange(tap_count, dtype=jnp.int32)[None, :]
    )
    frequency = first_bin + jnp.arange(bin_count, dtype=jnp.int32)
    phase_turns = jnp.mod(lag_index[:, :, None] * frequency[None, None, :], gate_len)
    phases = 2.0 * math.pi / gate_len * phase_turns.astype(jnp.float32)
    weight = jnp.where(lag_index >= 0, excitation[None, :], 0).astype(jnp.float32)[:, :, None]
    norm_scale = 1.0 / math.sqrt(tap_count * gate_len)
    real_part = jnp.sum(weight * jnp.cos(phases), axis=1) * norm_scale
    imag_part = -jnp.sum(weight * jnp.sin(phases), axis=1) * norm_scale
    return jnp.concatenate([real_part, imag_part], axis=1).astype(jnp.bfloat16)


def element_points(grid_cells, grid_rows):
    elem_x = (grid_cells[0].astype(jnp.float32) - 0.5 * (grid_rows - 1)) * pitch_mm
    elem_y = (grid_cells[1].astype(jnp.float32) - 15.5) * pitch_mm
    return (elem_x, elem_y)


def voxel_points(block_cells):
    cells_float = block_cells.astype(jnp.float32)
    return (
        (cells_float[0] - 31.5) * 0.5,
        (cells_float[1] - 31.5) * 0.5,
        10.0 + cells_float[2] * 0.5,
    )


def steer_angle(elem_x, elem_y, vox_x, vox_y, vox_z, frequency, gate_len):
    distance = jnp.sqrt(
        (elem_x[:, None] - vox_x[None, :]) ** 2
        + (elem_y[:, None] - vox_y[None, :]) ** 2
        + vox_z[None, :] ** 2
    )
    delay = distance * (samples_per_mm / gate_len)
    return 2.0 * math.pi * frequency.astype(jnp.float32)[:, None, None] * delay[None]


def general(captures, elem_grid, excitation, voxels):
    tx_count = lax.axis_size("tx")
    rx_count = lax.axis_size("rx")
    tx_rows, rx_cols, gate_len = captures.shape
    subrun = rx_cols // tx_count
    channels = 2 * BINS
    elements = tx_rows * tx_count
    matched = filter_table(excitation, gate_len, BINS)
    pieces = captures.reshape(rx_count, subrun, tx_count, subrun, gate_len)
    local_spec = jnp.einsum(
        "bhaxs,sc->cbhax", pieces, matched, preferred_element_type=jnp.float32
    ).astype(jnp.bfloat16)
    arrived = lax.all_to_all(
        lax.all_to_all(pieces, "tx", split_axis=2, concat_axis=2, tiled=True),
        "rx",
        split_axis=0,
        concat_axis=0,
        tiled=True,
    )
    mirror = jnp.einsum(
        "bhgxs,sc->cbxgh", arrived, matched, preferred_element_type=jnp.float32
    ).astype(jnp.bfloat16)
    averaged = ((local_spec.astype(jnp.float32) + mirror.astype(jnp.float32)) * 0.5).reshape(
        channels, tx_rows, rx_cols
    )
    power = jnp.mean(averaged * averaged, axis=0, keepdims=True)
    whitened = (
        (averaged / jnp.sqrt(jnp.maximum(power, power_floor)))
        .astype(jnp.bfloat16)
        .reshape(2, BINS, tx_rows, rx_cols)
    )
    left_side = jnp.concatenate([whitened[0], whitened[1]], axis=2)
    tx_cells = lax.dynamic_slice_in_dim(elem_grid, lax.axis_index("tx") * tx_rows, tx_rows, axis=1)
    rx_cells = lax.dynamic_index_in_dim(
        elem_grid.reshape(2, tx_count, rx_count, subrun),
        lax.axis_index("rx"),
        axis=2,
        keepdims=False,
    ).reshape(2, rx_cols)
    send_x, send_y = element_points(tx_cells, elements // 32)
    recv_x, recv_y = element_points(rx_cells, elements // 32)
    frequency = gate_len // 12 + jnp.arange(BINS, dtype=jnp.int32)
    voxel_count = voxels.shape[1]
    block_width = min(512, voxel_count)
    voxel_blocks = voxels.reshape(3, voxel_count // block_width, block_width).transpose(1, 0, 2)

    def image_block(block_cells):
        vox_x, vox_y, vox_z = voxel_points(block_cells)
        recv_phase = steer_angle(recv_x, recv_y, vox_x, vox_y, vox_z, frequency, gate_len)
        rx_cosine = jnp.cos(recv_phase).astype(jnp.bfloat16)
        rx_sine = jnp.sin(recv_phase).astype(jnp.bfloat16)
        steer_rx = jnp.concatenate(
            [
                jnp.concatenate([rx_cosine, rx_sine], axis=2),
                jnp.concatenate([-rx_sine, rx_cosine], axis=2),
            ],
            axis=1,
        )
        products = jnp.einsum(
            "ftl,flv->ftv", left_side, steer_rx, preferred_element_type=jnp.float32
        )
        prod_real = products[:, :, :block_width]
        prod_imag = products[:, :, block_width:]
        send_phase = steer_angle(send_x, send_y, vox_x, vox_y, vox_z, frequency, gate_len)
        tx_cosine = jnp.cos(send_phase)
        tx_sine = jnp.sin(send_phase)
        image_real = jnp.sum(prod_real * tx_cosine - prod_imag * tx_sine, axis=(0, 1))
        image_imag = jnp.sum(prod_real * tx_sine + prod_imag * tx_cosine, axis=(0, 1))
        return jnp.stack([image_real, image_imag])

    blocks = lax.map(image_block, voxel_blocks)
    partial_value = blocks.transpose(1, 0, 2).reshape(2, voxel_count) * (
        1.0 / (elements * math.sqrt(BINS))
    )
    image_part = lax.psum_scatter(partial_value, ("tx", "rx"), scatter_dimension=1, tiled=True)
    return image_part


def cosine_fit():
    grid = np.cos(np.pi * (np.arange(400) + 0.5) / 400) * 0.125 + 0.125
    fit = np.polynomial.chebyshev.Chebyshev.fit(
        grid, np.cos(2.0 * np.pi * np.sqrt(grid)), 8, domain=[0.0, 0.25]
    )
    return [float(c) for c in fit.convert(kind=np.polynomial.Polynomial).coef]


COSINE = cosine_fit()


def cos_turns(turns):
    rest = turns - jnp.floor(turns + 0.5)
    square = rest * rest
    total = jnp.full_like(square, COSINE[-1])
    for factor in COSINE[-2::-1]:
        total = total * square + factor
    return total


def iota(shape, axis):
    return lax.broadcasted_iota(jnp.int32, shape, axis)


def one_hot(mask):
    return jnp.where(mask, 1.0, 0.0).astype(jnp.bfloat16)


def matmul(left, right):
    return jnp.dot(left, right, preferred_element_type=jnp.float32)


def filter_lanes(taps, gate_len):
    first_bin = gate_len // 12

    def turns(rows):
        lane = iota((rows, LANES), 1)
        step = iota((rows, LANES), 0) * (first_bin + (lane & (BINS - 1)))
        return (step & (gate_len - 1)).astype(jnp.float32) * (1.0 / gate_len), lane

    tap_turns, _ = turns(taps)
    tables = jnp.concatenate([cos_turns(tap_turns), cos_turns(tap_turns - 0.25)], axis=1)
    high = tables.astype(jnp.bfloat16)
    rest = tables - high.astype(jnp.float32)
    middle = rest.astype(jnp.bfloat16)
    low = (rest - middle.astype(jnp.float32)).astype(jnp.bfloat16)
    reached = iota((gate_len, taps), 1) <= iota((gate_len, taps), 0)
    gate_turns, lane = turns(gate_len)
    gate_turns = gate_turns + jnp.where((lane & BINS) != 0, 0.25, 0.0)
    scale = 1.0 / math.sqrt(taps * gate_len)
    by_cosine = cos_turns(gate_turns) * scale
    by_sine = cos_turns(gate_turns - 0.25) * scale

    def table(excitation):
        weight = jnp.where(reached, excitation.astype(jnp.float32), 0.0).astype(jnp.bfloat16)
        sums = matmul(weight, high) + (matmul(weight, middle) + matmul(weight, low))
        return (by_cosine * sums[:, :LANES] + by_sine * sums[:, LANES:]).astype(jnp.bfloat16)

    return table


def steer_rows(elem_x, elem_y, points, gate_len, quarter, store):
    middle = gate_len // 12 + BINS // 2
    distance = jnp.sqrt(
        (elem_x - points[0]) ** 2 + (elem_y - points[1]) ** 2 + points[2] ** 2
    )
    turns = distance * (samples_per_mm / gate_len)
    twice = 2.0 * cos_turns(turns)
    for kind in range(2):
        back = 0.25 * kind
        now = cos_turns(turns * middle - back)
        before = cos_turns(turns * (middle - 1) - back)
        store(kind, BINS // 2, now)
        store(kind, BINS // 2 - 1, before)
        low, high = before, now
        for f in range(BINS // 2 - 2, -1, -1):
            low, high = twice * low - high, low
            store(kind, f, low)
        low, high = before, now
        for f in range(BINS // 2 + 1, BINS):
            low, high = high, twice * high - low
            store(kind, f, high)


def kernel(
    tx_count,
    rx_count,
    cap_any,
    grid_any,
    exc_any,
    vox_any,
    out_ref,
    cap,
    grid,
    exc,
    vox,
    steer_rx,
    steer_tx,
    send_spec,
    recv_spec,
    send_part,
    recv_part,
    load_sems,
    spec_sems,
    part_sems,
):
    devices = tx_count * rx_count
    tx_rows, rx_cols, gate_len = cap.shape
    subrun = rx_cols // tx_count
    channels = 2 * BINS
    width = subrun * subrun * channels
    voxel_count = vox.shape[1]
    owned = voxel_count // devices
    me_tx, me_rx = lax.axis_index("tx"), lax.axis_index("rx")
    me = me_tx * rx_count + me_rx
    slot = me_rx * tx_count + me_tx

    halves = [pl.ds(b * subrun, subrun) for b in range(rx_count)]
    pieces = [(cap_any.at[half], cap.at[half]) for half in halves]
    pieces += [(exc_any, exc), (grid_any, grid), (vox_any, vox)]
    loads = [
        pltpu.make_async_copy(source, target, load_sems.at[i])
        for i, (source, target) in enumerate(pieces)
    ]

    def place(other):
        return lax.div(other, rx_count), lax.rem(other, rx_count)

    def wait_rows(ref, semaphore, count, low=0, high=devices):
        if high - low > 1:
            middle = (low + high) // 2
            for side, span in ((count < middle, (low, middle)), (count >= middle, (middle, high))):

                @pl.when(side)
                def _(span=span):
                    wait_rows(ref, semaphore, count, *span)
        elif low:
            some = ref.at[pl.ds(0, low)]
            pltpu.make_async_copy(some, some, semaphore).wait()

    barrier = pltpu.get_barrier_semaphore()

    @pl.loop(me + 1, devices)
    def _(other):
        pl.semaphore_signal(
            barrier, inc=1, device_id=place(other), device_id_type=pl.DeviceIdType.MESH
        )

    for load in loads:
        load.start()

    make_table = filter_lanes(exc.shape[1], gate_len)
    pairs = subrun * rx_cols
    group = iota((pairs, width), 1) // channels
    outer = iota((pairs, width), 0) // rx_cols
    inner = iota((pairs, width), 0) & (subrun - 1)
    own_kept = group == subrun * outer + inner
    sent_kept = group == subrun * inner + outer
    pair = iota((tx_count, pairs), 1)
    gather = one_hot((pair & (rx_cols - 1)) // subrun == iota((tx_count, pairs), 0))
    loads[rx_count].wait()
    table = make_table(exc[...])
    table = jnp.concatenate([table] * (width // LANES), axis=1)
    own_spec = []
    for b in range(rx_count):
        loads[b].wait()
        spec = matmul(cap[halves[b]].reshape(pairs, gate_len), table)
        kept = [jnp.where(mask, spec, 0.0) for mask in (own_kept, sent_kept)]
        both = matmul(gather, jnp.concatenate(kept, axis=1).astype(jnp.bfloat16))
        own_spec.append(both[:, :width])
        send_spec[pl.ds(b * tx_count, tx_count)] = both[:, width:].reshape(tx_count, 1, width)
    own_spec = jnp.concatenate(own_spec, axis=0)
    recv_spec[pl.ds(slot, 1)] = send_spec[pl.ds(slot, 1)]

    @pl.when(me > 0)
    def _():
        pl.semaphore_wait(barrier, me)

    @pl.loop(0, me)
    def _(other):
        tx, rx = place(other)
        pltpu.make_async_remote_copy(
            src_ref=send_spec.at[rx * tx_count + tx],
            dst_ref=recv_spec.at[slot],
            send_sem=spec_sems.at[0],
            recv_sem=spec_sems.at[1],
            device_id=(tx, rx),
            device_id_type=pl.DeviceIdType.MESH,
        ).start()

    loads[rx_count + 1].wait()
    loads[rx_count + 2].wait()
    elements = grid.shape[1]
    cells = grid[...].astype(jnp.float32)
    x_line = (cells[0:1] - 0.5 * (elements // 32 - 1)) * pitch_mm
    y_line = (cells[1:2] - 15.5) * pitch_mm
    points = voxel_points(vox[...])
    points = tuple(p.reshape(1, voxel_count) for p in points)

    def columns(chosen):
        return (
            jnp.sum(jnp.where(chosen, x_line, 0.0), axis=1, keepdims=True),
            jnp.sum(jnp.where(chosen, y_line, 0.0), axis=1, keepdims=True),
        )

    chunk = 16
    for first in range(0, rx_cols, chunk):
        j = iota((chunk, elements), 0) + first
        element = (j // subrun) * tx_rows + me_rx * subrun + (j & (subrun - 1))
        elem_x, elem_y = columns(iota((chunk, elements), 1) == element)

        def store(kind, f, values, first=first):
            steer_rx[f, pl.ds(kind * rx_cols + first, chunk), :] = values.astype(jnp.bfloat16)

        steer_rows(elem_x, elem_y, points, gate_len, 0, store)
    element = iota((tx_rows, elements), 0) + me_tx * tx_rows
    elem_x, elem_y = columns(iota((tx_rows, elements), 1) == element)

    def store_tx(kind, f, values):
        steer_tx[f, pl.ds(kind * tx_rows, tx_rows), :] = values

    steer_rows(elem_x, elem_y, points, gate_len, 0, store_tx)

    same = one_hot(iota((width, width), 0) // channels == iota((width, width), 1) // channels)
    spread_rows = 2 * rx_cols
    spread = one_hot(
        iota((spread_rows, 2 * tx_count), 0) // subrun == iota((spread_rows, 2 * tx_count), 1)
    )
    long = rx_count * width
    kept = (iota((spread_rows, long), 1) // channels) % subrun == (
        iota((spread_rows, long), 0) & (subrun - 1)
    )
    fold_row = iota((channels * tx_rows, long), 0)
    fold_lane = iota((channels * tx_rows, long), 1)
    fold = one_hot(
        ((fold_row & (tx_rows - 1)) == fold_lane // (subrun * channels))
        & (fold_row // tx_rows == (fold_lane & (BINS - 1)) * 2 + ((fold_lane // BINS) & 1))
    )

    row = iota((devices, width), 0)
    sender = lax.rem(row, tx_count) * rx_count + lax.div(row, tx_count)
    times = jnp.where(sender > me, 2.0, 1.0)
    used = sender >= me
    imag_lane = (iota((devices, width), 1) & BINS) != 0

    wait_rows(recv_spec, spec_sems.at[1], devices - 1 - me)
    averaged = jnp.where(used, own_spec + recv_spec[...].reshape(devices, width), 0.0) * 0.5
    square = averaged * averaged
    high = square.astype(jnp.bfloat16)
    low = (square - high.astype(jnp.float32)).astype(jnp.bfloat16)
    power = (matmul(high, same) + matmul(low, same)) * (1.0 / channels)
    whitened = averaged * lax.rsqrt(jnp.maximum(power, power_floor)) * times
    turned = jnp.where(
        imag_lane, pltpu.roll(whitened, BINS, 1), -pltpu.roll(whitened, width - BINS, 1)
    )

    def side(values):
        return jnp.concatenate(
            [values[b * tx_count : (b + 1) * tx_count] for b in range(rx_count)], axis=1
        )

    both = jnp.concatenate([side(whitened), side(turned)], axis=0).astype(jnp.bfloat16)
    wide = jnp.where(kept, matmul(spread, both), 0.0).astype(jnp.bfloat16)
    left = lax.dot_general(
        fold, wide, (((1,), (1,)), ((), ())), preferred_element_type=jnp.float32
    ).astype(jnp.bfloat16)
    per_tile = LANES // owned
    scale = 1.0 / (elements * math.sqrt(BINS))
    tiles = voxel_count // LANES
    for first, last in ((0, 1), (1, tiles)):
        lanes = pl.ds(first * LANES, (last - first) * LANES)
        real = jnp.zeros((tx_rows, (last - first) * LANES), jnp.float32)
        imag = jnp.zeros_like(real)
        for f in range(BINS):
            products = matmul(
                left[2 * tx_rows * f : 2 * tx_rows * (f + 1)], steer_rx[f, :, lanes]
            )
            prod_real, prod_imag = products[:tx_rows], products[tx_rows:]
            tx_cosine = steer_tx[f, pl.ds(0, tx_rows), lanes]
            tx_sine = steer_tx[f, pl.ds(tx_rows, tx_rows), lanes]
            real += prod_real * tx_cosine - prod_imag * tx_sine
            imag += prod_real * tx_sine + prod_imag * tx_cosine
        image = jnp.concatenate(
            [jnp.sum(real, axis=0, keepdims=True), jnp.sum(imag, axis=0, keepdims=True)], axis=0
        )
        image = image * scale
        for tile in range(first, last):
            begin = (tile - first) * LANES
            send_part[tile] = image[:, begin : begin + LANES]

        @pl.loop(first * per_tile, last * per_tile)
        def _(other):
            @pl.when(other != me)
            def _():
                pltpu.make_async_remote_copy(
                    src_ref=send_part.at[lax.div(other, per_tile)],
                    dst_ref=recv_part.at[me],
                    send_sem=part_sems.at[0],
                    recv_sem=part_sems.at[1],
                    device_id=place(other),
                    device_id_type=pl.DeviceIdType.MESH,
                ).start()

    recv_part[pl.ds(me, 1)] = send_part[pl.ds(lax.div(me, per_tile), 1)]
    all_but_one = recv_part.at[pl.ds(0, devices - 1)]
    wait_rows(send_spec, spec_sems.at[0], me)
    for semaphore in range(2):
        pltpu.make_async_copy(all_but_one, all_but_one, part_sems.at[semaphore]).wait()
    total = jnp.sum(recv_part[...], axis=0)
    shift = lax.rem(LANES - owned * lax.rem(me, per_tile), LANES)
    out_ref[...] = pltpu.roll(total, shift, 1)[:, :owned]


def small(captures, elem_grid, excitation, voxels):
    tx_count = lax.axis_size("tx")
    rx_count = lax.axis_size("rx")
    devices = tx_count * rx_count
    tx_rows, rx_cols, gate_len = captures.shape
    voxel_count = voxels.shape[1]
    width = (rx_cols // tx_count) ** 2 * 2 * BINS
    excitation = excitation.reshape(1, -1)
    operands = [
        pltpu.with_memory_space_constraint(x, pltpu.HBM)
        for x in (captures, elem_grid, excitation, voxels)
    ]
    return pl.pallas_call(
        functools.partial(kernel, tx_count, rx_count),
        out_shape=pltpu.VMEM((2, voxel_count // devices), jnp.float32),
        in_specs=[pl.BlockSpec(memory_space=pltpu.HBM)] * 4,
        out_specs=pl.BlockSpec(memory_space=pltpu.VMEM),
        scratch_shapes=[
            pltpu.VMEM(captures.shape, captures.dtype),
            pltpu.VMEM(elem_grid.shape, jnp.int32),
            pltpu.VMEM(excitation.shape, jnp.int32),
            pltpu.VMEM(voxels.shape, jnp.int32),
            pltpu.VMEM((BINS, 2 * rx_cols, voxel_count), jnp.bfloat16),
            pltpu.VMEM((BINS, 2 * tx_rows, voxel_count), jnp.float32),
            pltpu.VMEM((devices, 1, width), jnp.float32),
            pltpu.VMEM((devices, 1, width), jnp.float32),
            pltpu.VMEM((voxel_count // LANES, 2, LANES), jnp.float32),
            pltpu.VMEM((devices, 2, LANES), jnp.float32),
            pltpu.SemaphoreType.DMA((rx_count + 3,)),
            pltpu.SemaphoreType.DMA((2,)),
            pltpu.SemaphoreType.DMA((2,)),
        ],
        compiler_params=pltpu.CompilerParams(
            collective_id=0, has_side_effects=True, vmem_limit_bytes=32 * 1024 * 1024
        ),
    )(*operands)


def local(captures, elem_grid, excitation, voxels):
    tx_count = lax.axis_size("tx")
    devices = tx_count * lax.axis_size("rx")
    tx_rows, rx_cols, _ = captures.shape
    fits = (
        tx_rows == 8
        and rx_cols == 64
        and rx_cols // tx_count == 4
        and voxels.shape[1] <= 1024
        and LANES % (voxels.shape[1] // devices) == 0
    )
    return (small if fits else general)(captures, elem_grid, excitation, voxels)


def solution(mesh):
    placed = (P("tx", "rx", None), P(), P(), P())
    return jax.shard_map(
        local, mesh=mesh, in_specs=placed, out_specs=P(None, ("tx", "rx")), check_vma=False
    )
```
